32 devices in a mesh: row: 8 (over y, x, core), col: 4 (over z).
Axes of the slice: x: 2, y: 2, z: 4, core: 2. Of those that a mesh axis runs over, the one named last changes fastest.
Arguments:
- documents: bfloat16 [2, 4096, 2048], P(None, ('row', 'col')), may hold values from -6 to 6
- targets: bfloat16 [2, 4096, 2048], P(None, ('row', 'col')), may hold values from -6 to 6
- routes: int32 [2, 4096, 1], P(None, ('row', 'col')), may hold values from 0 to 31; in each aligned block of 128 rows (0 to 127, 128 to 255, ..., all dimensions but the last counted through in order) at most 8 rows name the same one
- doc_counts: int32 [8, 4], replicated, may hold values from 1 to 64
- module_one: float32 [8, 2048, 2048], P('row', 'col'), may hold values from -6 to 6
- module_two: float32 [4, 2048, 2048], P('col', 'row'), may hold values from -6 to 6
- moment_one: float32 [8, 2048, 2048], P('row', 'col'), may hold values from -0.75 to 0.75
- moment_two: float32 [4, 2048, 2048], P('col', 'row'), may hold values from -0.75 to 0.75
Outputs:
- new_one: float32 [8, 2048, 2048], P('row', 'col')
- new_two: float32 [4, 2048, 2048], P('col', 'row')
- next_moment_one: float32 [8, 2048, 2048], P('row', 'col')
- next_moment_two: float32 [4, 2048, 2048], P('col', 'row')
The draws below stay inside these ranges and needn't reach their ends.
Inputs may be any that keep to these rules, and one draw needn't show every extreme that they name: `routes`: in each micro-batch, at most 8 of the 128 rows that one device holds name the same path.
All inputs are finite; a program needn't handle non-finite values.
Results may differ from the reference program's by a relative error of at most 0.011.
Values may be sent and summed in bfloat16 or wider, within the bound.
No kernel may reach another device: no remote copies, remote signals or barrier semaphores. Data moves between devices by JAX's collectives and lax.ppermute only.
A program may use at most 192 MiB of HBM per device.

```python
import math
import jax
import jax.numpy as jnp
import numpy as np
from jax import lax

D = 2048
ROWS_DEV = 128
MICRO = 2
PATHS = 32
CAP = 8
TOKENS = 4096
N_ROW = 8
N_COL = 4


def place_ends(drawn, rng, smallest, largest):
    spot = [jax.random.randint(jax.random.fold_in(rng, axis), (), 0, length) for axis, length in enumerate(drawn.shape)]
    widest = drawn.shape.index(max(drawn.shape))
    next_to = spot[:widest] + [(spot[widest] + 1) % drawn.shape[widest]] + spot[widest + 1:]
    return drawn.at[tuple(spot)].set(smallest).at[tuple(next_to)].set(largest)


def level_of(key, dims, split, smallest, top_value):
    factor_of, own = 1.0, jax.random.fold_in(key, 6)
    for dim, parts in split:
        heights = jnp.exp(jax.random.uniform(jax.random.fold_in(own, dim), (parts,), jnp.float32, smallest / len(split), top_value / len(split)))
        factor_of = factor_of * jnp.repeat(heights, dims[dim] // parts).reshape([-1 if axis == dim else 1 for axis in range(len(dims))])
    return factor_of


def shared_out(stream_key, own, number, rows, amount, top, bound, slope):
    order = jax.random.permutation(stream_key, amount)
    crowded, ordinary = load_shares(amount, rows * top, bound, slope, True), load_shares(amount, rows * top, bound, slope, False)
    places = jnp.arange(amount)

    def named(lengths, offset_by):
        used = int((lengths > 0).sum())
        fixed = max(1, used // 4)
        moved = fixed + (places - fixed + offset_by * (used - fixed)) % max(1, amount - fixed)
        return jnp.zeros((amount,), jnp.int32).at[order[jnp.where(places < fixed, places, moved)]].set(jnp.asarray(lengths, jnp.int32))

    lengths = jnp.where(number % 4 == 0, named(crowded, number // 4), named(ordinary, number - number // 4 - 1))
    mixed = jax.random.permutation(jax.random.fold_in(own, 3), amount)
    source_of, receiver = mixed[0:amount // 2 * 2:2], mixed[1:amount // 2 * 2:2]
    room = jnp.minimum(lengths[source_of] - 1, bound - lengths[receiver]) // 2
    room = jnp.where((source_of == order[0]) | (receiver == order[0]) | (lengths[receiver] == 0), 0, jnp.maximum(room, 0))
    moved = jax.random.randint(jax.random.fold_in(own, 4), (amount // 2,), 0, 1 << 20) % (room + 1)
    lengths = lengths.at[source_of].add(-moved).at[receiver].add(moved)
    labels = jnp.searchsorted(jnp.cumsum(lengths), jnp.arange(rows * top), side="right").astype(jnp.int32)
    grid = labels.reshape(top, rows).T
    grid = grid[jax.random.permutation(jax.random.fold_in(own, 1), rows)]
    offset_by = jax.random.randint(jax.random.fold_in(own, 2), (rows, 1), 0, top)
    return jnp.take_along_axis(grid, (jnp.arange(top)[None, :] + offset_by) % top, axis=1)


def load_shares(number_of, total, limit, lean, full):
    loads = [(1 << 20) // math.isqrt(standing ** lean) + 1 for standing in range(1, number_of + 1)]
    largest = limit if full else min(limit, max(-(-total // number_of), total * loads[0] // sum(loads)))
    least = 1 if total - largest >= number_of - 1 else 0
    holding, rest = [largest] + [least] * (number_of - 1), total - largest - least * (number_of - 1)
    while rest > 0:
        candidates = [i for i in range(1, number_of) if holding[i] < largest] or [i for i in range(1, number_of) if holding[i] < limit]
        whole, left = sum([loads[i] for i in candidates]), rest
        for i in candidates:
            addition = min(limit - holding[i], max(1, left * loads[i] // whole), rest)
            holding[i] = holding[i] + addition
            rest = rest - addition
    return np.array(holding)


def bell_draw(key, shape, scale, reach, shards=(), held_as=jnp.bfloat16):
    drawn = jax.random.normal(key, shape, jnp.float32) * scale
    if len(shards) > 0:
        drawn = level_of(key, shape, shards, -0.22, 0.18) * drawn
    return jnp.clip(drawn, min=-reach, max=reach).astype(held_as)


def setup_inputs(seed: int = 0) -> dict:
    key_list = jax.random.split(jax.random.key(seed), 9)
    documents = bell_draw(key_list[0], (MICRO, TOKENS, D), 1.0, 6.0, ((1, 32),))
    targets = bell_draw(key_list[1], (MICRO, TOKENS, D), 1.0, 6.0, ((1, 32),))
    routes_keys = jax.random.split(jax.random.fold_in(key_list[2], 1), MICRO * TOKENS // ROWS_DEV)
    routes_turns = jax.random.permutation(jax.random.fold_in(key_list[2], 3), MICRO * TOKENS // ROWS_DEV)
    routes = jax.vmap(lambda own, number: shared_out(jax.random.fold_in(key_list[2], 2), own, number, ROWS_DEV, PATHS, 1, CAP, 2))(routes_keys, routes_turns).reshape((MICRO, TOKENS, 1))
    doc_counts = place_ends(jax.random.randint(key_list[3], (N_ROW, N_COL), 1, 65), jax.random.fold_in(key_list[3], 1), 1, 64).astype(jnp.int32)
    module_one = bell_draw(key_list[4], (N_ROW, D, D), 1.0, 6.0, ((0, 8), (1, 4)), jnp.float32)
    module_two = bell_draw(key_list[5], (N_COL, D, D), 1.0, 6.0, ((0, 4), (1, 8)), jnp.float32)
    moment_one = bell_draw(key_list[6], (N_ROW, D, D), 0.05, 0.75, ((0, 8), (1, 4)), jnp.float32)
    moment_two = bell_draw(key_list[7], (N_COL, D, D), 0.05, 0.75, ((0, 4), (1, 8)), jnp.float32)
    return dict(documents=documents, targets=targets, routes=routes, doc_counts=doc_counts, module_one=module_one, module_two=module_two, moment_one=moment_one, moment_two=moment_two)


beta_one = 0.9
beta_two = 0.95
inner_rate = 0.1
decay = 0.1
outer_rate = 0.7
outer_moment = 0.9

def silu_slope(pre):
    sig = jax.nn.sigmoid(pre)
    return sig * (1.0 + pre * (1.0 - sig))

def gradients(w_one, w_two, rows, targs, valid):
    scale = D ** (-0.5)
    pre = jnp.dot(rows, w_one, preferred_element_type=jnp.float32) * scale
    hidden = jax.nn.silu(pre).astype(jnp.bfloat16)
    out = rows.astype(jnp.float32) + jnp.dot(hidden, w_two, preferred_element_type=jnp.float32) * scale
    error = ((out - targs.astype(jnp.float32)) * valid / ROWS_DEV).astype(jnp.bfloat16)
    grad_two = lax.dot_general(hidden, error, (((0,), (0,)), ((), ())), preferred_element_type=jnp.float32) * scale
    back = lax.dot_general(error, w_two, (((1,), (1,)), ((), ())), preferred_element_type=jnp.float32) * scale
    inner = (back * silu_slope(pre)).astype(jnp.bfloat16)
    grad_one = lax.dot_general(rows, inner, (((0,), (0,)), ((), ())), preferred_element_type=jnp.float32) * scale
    return (grad_one, grad_two)

def adamw(param, grad, first, second, step, guard):
    first = beta_one * first + (1.0 - beta_one) * grad
    second = beta_two * second + (1.0 - beta_two) * grad * grad
    fix_one = 1.0 - beta_one ** (step + 1)
    fix_two = 1.0 - beta_two ** (step + 1)
    update = first / fix_one / (jnp.sqrt(second / fix_two) + guard) + decay * param
    return (param - inner_rate * update, first, second)

def train_path(start_one, start_two, documents, targets, routes, path):
    slots = N_ROW * N_COL * CAP
    guard = 0.5 / (D * ROWS_DEV) ** 0.5
    p_one = start_one.astype(jnp.float32)
    p_two = start_two.astype(jnp.float32)
    m_one = jnp.zeros_like(p_one)
    v_one = jnp.zeros_like(p_one)
    m_two = jnp.zeros_like(p_two)
    v_two = jnp.zeros_like(p_two)
    for step in range(MICRO):
        dest = routes[step, :, 0]
        order = jnp.argsort((dest != path).astype(jnp.int32), stable=True)[:slots]
        hit = jnp.take(dest, order) == path
        valid = hit.astype(jnp.float32)[:, None]
        rows = jnp.where(hit[:, None], jnp.take(documents[step], order, axis=0), jnp.zeros((), jnp.bfloat16))
        targs = jnp.where(hit[:, None], jnp.take(targets[step], order, axis=0), jnp.zeros((), jnp.bfloat16))
        grad_one, grad_two = gradients(p_one.astype(jnp.bfloat16), p_two.astype(jnp.bfloat16), rows, targs, valid)
        p_one, m_one, v_one = adamw(p_one, grad_one, m_one, v_one, step, guard)
        p_two, m_two, v_two = adamw(p_two, grad_two, m_two, v_two, step, guard)
    return (start_one.astype(jnp.float32) - p_one, start_two.astype(jnp.float32) - p_two)

def rounded(value):
    return lax.optimization_barrier(value.astype(jnp.bfloat16)).astype(jnp.float32)

def reference(documents, targets, routes, doc_counts, module_one, module_two, moment_one, moment_two):
    counts = doc_counts.astype(jnp.float32)
    weight_one = counts / lax.optimization_barrier(jnp.sum(counts, axis=1, keepdims=True))
    weight_two = counts / lax.optimization_barrier(jnp.sum(counts, axis=0, keepdims=True))
    start_one_all = module_one.astype(jnp.bfloat16)
    start_two_all = module_two.astype(jnp.bfloat16)

    def visit(carry, path):
        sum_one, sum_two = carry
        index_one = (path // N_COL).astype(jnp.int32)
        index_two = (path % N_COL).astype(jnp.int32)
        start_one = lax.dynamic_index_in_dim(start_one_all, index_one, 0, keepdims=False)
        start_two = lax.dynamic_index_in_dim(start_two_all, index_two, 0, keepdims=False)
        delta_one, delta_two = train_path(start_one, start_two, documents, targets, routes, path)
        term_one = rounded(weight_one[index_one, index_two] * delta_one)
        term_two = rounded(weight_two[index_one, index_two] * delta_two)
        sum_one = sum_one.at[index_one].add(term_one)
        sum_two = sum_two.at[index_two].add(term_two)
        return ((sum_one, sum_two), None)
    init = (jnp.zeros(module_one.shape, jnp.float32), jnp.zeros(module_two.shape, jnp.float32))
    (avg_one, avg_two), unused = lax.scan(visit, init, jnp.arange(N_ROW * N_COL, dtype=jnp.int32))
    next_moment_one = outer_moment * moment_one + avg_one
    next_moment_two = outer_moment * moment_two + avg_two
    new_one = module_one - outer_rate * (outer_moment * next_moment_one + avg_one)
    new_two = module_two - outer_rate * (outer_moment * next_moment_two + avg_two)
    return (new_one, new_two, next_moment_one, next_moment_two)
```

```python
import functools

import jax
import jax.numpy as jnp
from jax import lax
from jax.experimental import pallas as pl
from jax.experimental.pallas import tpu as pltpu
from jax.sharding import PartitionSpec as P

beta_one = 0.9
beta_two = 0.95
inner_rate = 0.1
decay = 0.1
outer_rate = 0.7
outer_moment = 0.9

VMEM_LIMIT = 56 * 1024 * 1024
f32 = jnp.float32
bf16 = jnp.bfloat16


def step_kernel(rows_dev, tile, keep, base, one_at, two_at, *refs):
    n_one, n_two = len(one_at), len(two_at)
    place_ref, xy_ref = refs[:2]
    refs = refs[2:]

    def take(places):
        nonlocal refs
        found = [tuple(refs[sum(p[1] for p in places[:i]) :][: p[1]]) for i, p in enumerate(places)]
        refs = refs[sum(p[1] for p in places) :]
        return found

    one_refs, two_refs = take(one_at), take(two_at)
    left_ref, right_ref = refs[:2]
    start_out = refs[2] if keep else None
    one, two, pre, one_sem, two_sem, out_sem = refs[-6:]
    width = one.shape[0]
    scale = width ** (-0.5)
    parts = width // tile
    home = place_ref[base + n_one + n_two]

    class Copies:
        def __init__(self, *choices):
            self.choices = choices

        def start(self):
            if len(self.choices) == 1:
                self.choices[0].start()
            else:
                pl.when(home == 1)(self.choices[0].start)
                pl.when(home == 0)(self.choices[1].start)

        def wait(self):
            self.choices[0].wait()

    def one_copies(n):
        found = []
        for i, (pieces, (first, _, top, tall)) in enumerate(zip(one_refs, one_at)):
            wide = pieces[0].shape[1]
            if first <= n * tile < first + wide:
                down = pl.ds(pl.multiple_of(place_ref[base + i] * tall, tall), tall)
                found.append(
                    Copies(*[
                        pltpu.make_async_copy(
                            piece.at[pl.ds(top, tall), pl.ds(n * tile - first, tile)],
                            one.at[down, pl.ds(n * tile, tile)],
                            one_sem.at[i, n],
                        )
                        for piece in pieces
                    ])
                )
        return found

    two_copies = []
    for i, (pieces, (first, _, top, tall)) in enumerate(zip(two_refs, two_at)):
        wide = pieces[0].shape[1]
        down = pl.ds(pl.multiple_of(place_ref[base + n_one + i] * tall, tall), tall)
        two_copies.append(
            Copies(*[
                pltpu.make_async_copy(piece.at[pl.ds(top, tall), :], two.at[down, pl.ds(first, wide)], two_sem.at[i])
                for piece in pieces
            ])
        )
    for n in range(parts):
        for copy in one_copies(n):
            copy.start()
    for copy in two_copies:
        copy.start()
    for n in range(parts):
        span = pl.ds(n * tile, tile)
        for copy in one_copies(n):
            copy.wait()
        value = jnp.dot(xy_ref[:, :width], one[:, span], preferred_element_type=f32) * scale
        pre[:, span] = value
        left_ref[:, span] = xy_ref[:, span]
        left_ref[:, pl.ds(width + n * tile, tile)] = (value * jax.nn.sigmoid(value)).astype(bf16)
    for copy in two_copies:
        copy.wait()
    if keep:
        one_save = pltpu.make_async_copy(one, start_out.at[pl.ds(0, width), :], out_sem.at[0])
        two_save = pltpu.make_async_copy(two, start_out.at[pl.ds(width, width), :], out_sem.at[1])
        one_save.start()
        two_save.start()

    def miss(n, carry):
        span = pl.ds(pl.multiple_of(n * tile, tile), tile)
        late = pl.ds(pl.multiple_of(width + n * tile, tile), tile)
        out = xy_ref[:, span].astype(f32) + jnp.dot(left_ref[:, width:], two[:, span], preferred_element_type=f32) * scale
        right_ref[:, late] = ((out - xy_ref[:, late].astype(f32)) / rows_dev).astype(bf16)
        return carry

    lax.fori_loop(0, parts, miss, 0)

    def backward(n, carry):
        span = pl.ds(pl.multiple_of(n * tile, tile), tile)
        back = lax.dot_general(
            right_ref[:, width:], two[span, :], (((1,), (1,)), ((), ())), preferred_element_type=f32
        ) * scale
        value = pre[:, span]
        sig = jax.nn.sigmoid(value)
        right_ref[:, span] = (back * (sig * (1.0 + value * (1.0 - sig)))).astype(bf16)
        return carry

    lax.fori_loop(0, parts, backward, 0)
    if keep:
        one_save.wait()
        two_save.wait()


def step(xy, one, two, rows_dev, keep, places, base):
    rows, width = xy.shape[0], xy.shape[1] // 2
    tile = 512
    vmem = pl.BlockSpec(memory_space=pltpu.VMEM)
    hbm = pl.BlockSpec(memory_space=pl.ANY)
    out = jax.ShapeDtypeStruct((rows, 2 * width), bf16)
    whole = jax.ShapeDtypeStruct((2 * width, width), bf16)
    sources = [array for p in one + two for array in p[0]]

    def entries(pieces):
        return tuple((p[1], len(p[0]), *(p[2:] or (0, p[0][0].shape[0]))) for p in pieces)

    return pl.pallas_call(
        functools.partial(
            step_kernel, rows_dev, tile, keep, base, entries(one), entries(two)
        ),
        out_shape=(out, out) + ((whole,) if keep else ()),
        in_specs=[pl.BlockSpec(memory_space=pltpu.SMEM), vmem] + [hbm] * len(sources),
        out_specs=(vmem, vmem) + ((hbm,) if keep else ()),
        scratch_shapes=[
            pltpu.VMEM((width, width), bf16),
            pltpu.VMEM((width, width), bf16),
            pltpu.VMEM((rows, width), f32),
            pltpu.SemaphoreType.DMA((len(one), width // tile)),
            pltpu.SemaphoreType.DMA((len(two),)),
            pltpu.SemaphoreType.DMA((2,)),
        ],
        compiler_params=pltpu.CompilerParams(vmem_limit_bytes=VMEM_LIMIT),
        cost_estimate=pl.CostEstimate(flops=15 * rows * width * width, bytes_accessed=4 * width * width, transcendentals=0),
    )(places, xy, *sources)


def update_kernel(guard, tile, a_ref, b_ref, p_ref, out_ref):
    shrink = inner_rate * decay
    turned = a_ref[...].T
    for n in range(p_ref.shape[1] // tile):
        span = slice(n * tile, (n + 1) * tile)
        grad = jnp.dot(turned, b_ref[:, span], preferred_element_type=f32)
        move = grad * pl.reciprocal(jnp.abs(grad) + guard, approx=True)
        out_ref[:, span] = (p_ref[:, span].astype(f32) * (1.0 - shrink) - inner_rate * move).astype(bf16)


def update(left, right, start, guard):
    rows, width = left.shape[0], start.shape[1]
    tall = 512
    each = width // tall
    return pl.pallas_call(
        functools.partial(update_kernel, guard * width ** 0.5, 512),
        out_shape=jax.ShapeDtypeStruct(start.shape, bf16),
        grid=(2 * each,),
        in_specs=[
            pl.BlockSpec((rows, tall), lambda m: (0, m)),
            pl.BlockSpec((rows, width), lambda m: (0, m // each)),
            pl.BlockSpec((tall, width), lambda m: (m, 0)),
        ],
        out_specs=pl.BlockSpec((tall, width), lambda m: (m, 0)),
        compiler_params=pltpu.CompilerParams(vmem_limit_bytes=VMEM_LIMIT),
        cost_estimate=pl.CostEstimate(flops=12 * rows * width * start.shape[0], bytes_accessed=4 * start.size, transcendentals=0),
    )(left, right, start)


def term_kernel(guard, tile, base, spans, place_ref, weight_ref, a_ref, b_ref, c_ref, d_ref, p_ref, *refs):
    outs, held, sem = refs[:-2], refs[-2], refs[-1]
    step = pl.program_id(0)
    slot = step % 2
    last = spans[-1][1]
    short, wide = p_ref.shape

    def copies(m, slot):
        return [
            (
                (m >= begin) & (m < end),
                pltpu.make_async_copy(
                    held.at[slot], out.at[pl.ds(pl.multiple_of((m - begin) * short, short), short), :], sem.at[slot]
                ),
            )
            for out, (begin, end) in zip(outs, spans)
        ]

    def settle(slot):
        pltpu.make_async_copy(held.at[slot], outs[0].at[pl.ds(0, short), :], sem.at[slot]).wait()

    @pl.when(step >= 2)
    def _():
        settle(slot)

    weight = jnp.where(place_ref[base + 3 * last + step] == 0, weight_ref[0], weight_ref[1])
    shrink = inner_rate * decay
    new_m = (1.0 - beta_one) / (1.0 - beta_one ** 2)
    new_v = ((1.0 - beta_two) / (1.0 - beta_two ** 2)) ** 0.5
    by_first = weight * (inner_rate * (1.0 - shrink))
    by_second = weight * (inner_rate * new_m / new_v)
    by_start = weight * (shrink * (2.0 - shrink))
    older, newer = a_ref[...].T, c_ref[...].T
    for n in range(wide // tile):
        span = slice(n * tile, (n + 1) * tile)
        old = jnp.dot(older, b_ref[:, span], preferred_element_type=f32)
        new = jnp.dot(newer, d_ref[:, span], preferred_element_type=f32)
        first = old * pl.reciprocal(jnp.abs(old) + guard, approx=True)
        square = beta_two * (old * old) + new * new
        root = square * lax.rsqrt(square + 1e-30)
        second = (beta_one * old + new) * pl.reciprocal(root + guard / new_v, approx=True)
        start = p_ref[:, span].astype(f32)
        held[slot, :, span] = (first * by_first + second * by_second + start * by_start).astype(bf16)
    for here, copy in copies(step, slot):
        pl.when(here)(copy.start)

    @pl.when(step == last - 1)
    def _():
        settle(slot)
        if last > 1:
            settle(1 - slot)


def terms(weights, places, base, counts, short, parts, a, b, c, d, p, guard):
    rows, width = a.shape[0], p.shape[1]
    wide = width // parts
    ends = [sum(counts[: n + 1]) for n in range(len(counts))]
    spans = tuple((end - count, end) for count, end in zip(counts, ends))
    last = ends[-1]
    row = lambda m, at: at[base + m]
    col = lambda m, at: at[base + last + m]
    both = lambda m, at: at[base + 2 * last + m]
    side = pl.BlockSpec((rows, short), lambda m, at: (0, row(m, at)))
    full = pl.BlockSpec((rows, wide), lambda m, at: (0, both(m, at)))
    return pl.pallas_call(
        functools.partial(term_kernel, guard * width ** 0.5, 256, base, spans),
        out_shape=tuple(jax.ShapeDtypeStruct((count * short, wide), bf16) for count in counts),
        grid_spec=pltpu.PrefetchScalarGridSpec(
            num_scalar_prefetch=1,
            grid=(last,),
            in_specs=[
                pl.BlockSpec(memory_space=pltpu.SMEM),
                side, full, side, full,
                pl.BlockSpec((short, wide), lambda m, at: (row(m, at), col(m, at))),
            ],
            out_specs=tuple(pl.BlockSpec(memory_space=pl.ANY) for _ in counts),
            scratch_shapes=[pltpu.VMEM((2, short, wide), bf16), pltpu.SemaphoreType.DMA((2,))],
        ),
        compiler_params=pltpu.CompilerParams(vmem_limit_bytes=VMEM_LIMIT),
        cost_estimate=pl.CostEstimate(flops=1, bytes_accessed=1, transcendentals=0),
    )(places, weights, a, b, c, d, p)


def slots(routes, documents, targets, device_of, room):
    dest = device_of(routes[:, 0])
    paths = device_of(None)
    hit = (dest[:, None] == jnp.arange(paths, dtype=jnp.int32)[None, :]).astype(jnp.int32)
    before = jnp.cumsum(hit, axis=0) - hit
    slot = dest * room + jnp.sum(before * hit, axis=1)
    place = (slot[:, None] == jnp.arange(paths * room, dtype=jnp.int32)[None, :]).astype(bf16)
    both = jnp.concatenate([documents, targets], axis=1)
    return jnp.einsum("rs,rd->sd", place, both, preferred_element_type=f32).astype(bf16)


def after(value, *others):
    return lax.optimization_barrier((value,) + others)[0]


def shards(documents, targets, routes, doc_counts, module_one, module_two, moment_one, moment_two):
    n_row = lax.axis_size("row")
    n_col = lax.axis_size("col")
    chips, half = n_row // 2, n_col // 2
    paths = n_row * n_col
    row_id = lax.axis_index("row")
    col_id = lax.axis_index("col")
    chip, core = row_id // 2, row_id % 2
    side, turn = col_id // half, col_id % half
    home = core == side
    micro, rows_dev, width = documents.shape
    room = max(2, 2 * rows_dev // paths)
    guard = 0.5 / (width * rows_dev) ** 0.5

    def device_of(path):
        if path is None:
            return paths
        i, j = path // n_col, path % n_col
        return (2 * (i // 2) + j // half) * n_col + (i % 2) * half + j % half

    def send(value, target):
        pairs = []
        for i in range(n_row):
            for k in range(n_col):
                to = target(i // 2, i % 2, k // half, k % half)
                if to is not None:
                    c, b, h, q = to
                    pairs.append((i * n_col + k, (2 * c + b) * n_col + h * half + q))
        return lax.ppermute(value, ("row", "col"), pairs)

    def to_core(value):
        return send(value, lambda c, b, h, q: (c, 1 - b, h, q))

    def to_turn(value, s):
        return send(value, lambda c, b, h, q: (c, b, h, (q + s) % half))

    def to_chip(value, bit):
        return send(value, lambda c, b, h, q: (c ^ bit, b, h, q))

    bits = [1 << t for t in range(chips.bit_length() - 1)]
    orders = [bits, bits[::-1]]
    cols = width // 2

    every = list(range(chips))
    tall_one, tall_two = width // n_col, width // chips
    short = min(tall_one, tall_two, 512)
    table = []

    def enter(*pieces):
        talls = (tall_one, tall_two)
        listed = [
            (
                level * (width // short) + block * (talls[level] // short) + cut,
                part,
                level * 2 + part,
                level,
            )
            for level, blocks, part in pieces
            for block in blocks
            for cut in range(talls[level] // short)
        ]
        base = len(table)
        for field in zip(*listed):
            table.extend(field)
        return base, tuple(len(blocks) * (talls[level] // short) for level, blocks, part in pieces)

    here = [(turn + s) % half + core * half for s in range(half)]
    there = [(turn + s) % half + (1 - core) * half for s in range(half)]
    leave = [[chip ^ r for r in every if r & order[0]] for order in orders]
    stay = [[chip ^ r for r in every if not r & order[0]] for order in orders]
    calls = [
        enter((0, there, 0), (0, there, 1)),
        enter((0, here, 0), (0, here, 1)),
        enter((1, leave[0], 0), (1, leave[1], 1)),
        enter((1, stay[0], 0), (1, stay[1], 1)),
    ]
    base_first = len(table)
    for part in range(2):
        for s in range(half):
            table += [(turn - s) % half + core * half, (turn - s) % half + (1 - core) * half]
    table += [chip ^ r for part in range(2) for r in every] + [home]
    base_second = len(table)
    table += [0, 0, 0]
    places = jnp.stack([jnp.asarray(value).astype(jnp.int32) for value in table])

    counts = doc_counts.astype(f32)
    path_one, path_two = 2 * chip + side, turn + core * half
    in_row = (jnp.arange(n_row) == path_one)[:, None]
    in_col = (jnp.arange(n_col) == path_two)[None, :]
    row_counts = jnp.sum(jnp.where(in_row, counts, 0.0))
    col_counts = jnp.sum(jnp.where(in_col, counts, 0.0))
    own_count = jnp.sum(jnp.where(in_row & in_col, counts, 0.0))
    weights = jnp.stack([own_count / row_counts, own_count / col_counts])

    sent = [slots(routes[s], documents[s], targets[s], device_of, room) for s in range(micro)]

    def exchange(value):
        return lax.all_to_all(
            value.reshape(paths, room, 2 * width), ("row", "col"), split_axis=0, concat_axis=0, tiled=True
        ).reshape(paths * room, 2 * width)

    own_two = module_two[0].astype(bf16)
    own_one = module_one[0].astype(bf16)
    other_two = send(own_two, lambda c, b, h, q: (c, h, h, q) if b != h else None)
    pair_two = jnp.where(
        core == 0,
        jnp.concatenate([own_two, other_two], axis=0),
        jnp.concatenate([other_two, own_two], axis=0),
    )
    pair_two = [pair_two[:, :cols], pair_two[:, cols:]]

    def far_two(part, *others):
        return send(after(pair_two[part], *others), lambda c, b, h, q: (c, b, 1 - h, q) if b == h else None)

    def spread(held, bit, here):
        return held | {
            r ^ bit: send(value, lambda c, b, h, q: (c ^ bit, b, h, q) if (b == h) == here else None)
            for r, value in sorted(held.items())
        }

    def rest(held, here):
        for n in range(1, len(bits)):
            held = [spread(held[part], orders[part][n], here) for part in range(2)]
        return held

    def values(held):
        return [value for part in held for value in part.values()]

    ones = [own_one[:, :cols], own_one[:, cols:]]

    def shift(value, here):
        if half == 1:
            return jnp.zeros_like(value)
        return send(value, lambda c, b, h, q: (c, b, h, (q + 1) % half) if (b == h) == here else None)

    def far_one(part, *others):
        return send(
            after(ones[part], *others), lambda c, b, h, q: (c, 1 - b, 1 - h, q) if b != h else None
        )

    got_a = exchange(sent[0])
    shift_a = shift(ones[0], True)
    shift_b = shift(ones[1], True)
    home_two = [spread({0: pair_two[part]}, orders[part][0], True) for part in range(2)]
    home_two = rest(home_two, True)
    far_a = far_two(0)
    far_b = far_two(1)
    first = (got_a, shift_a, shift_b, far_a, far_b, *values(home_two))
    away_two = [spread({0: far}, orders[part][0], False) for part, far in enumerate((far_a, far_b))]
    one_a = far_one(0, *first)
    one_b = far_one(1, one_a, *values(away_two), places, weights, *sent[1:])
    turn_a = shift(one_a, False)
    away_two = rest(away_two, False)
    turn_b = shift(after(one_b, turn_a, *values(away_two)), False)
    one = []
    for part, (own, far, near, turned) in enumerate(
        ((ones[0], one_a, shift_a, turn_a), (ones[1], one_b, shift_b, turn_b))
    ):
        first = jnp.where(home, own, far)
        held = [first]
        if half > 1:
            held.append(jnp.where(home, near, turned))
        held += [to_turn(first, s) for s in range(2, half)]
        for value in held:
            one.append(((value,), part * cols))
            one.append(((to_core(value),), part * cols))
    two = [((home_two[part][r], away_two[part][r]), part * cols) for part in range(2) for r in every]
    got_b = exchange(after(sent[1], got_a, *[p[0][0] for p in one + two]))
    left_a, right_a, start = step(got_a, one, two, rows_dev, True, places, base_first)
    moved = update(left_a, right_a, start, guard)
    left_b, right_b = step(got_b, [((moved,), 0, 0, width)], [((moved,), 0, width, width)], rows_dev, False, places, base_second)

    def deltas(call, *others):
        return terms(after(weights, *others), places, *call, short, 2, left_a, right_a, left_b, right_b, start, guard)

    def summed(*values):
        return functools.reduce(lambda x, y: x + y, [value.astype(f32) for value in values])

    def both_cores(here, there):
        there = to_core(there)
        cuts = [slice(s * tall_one, (s + 1) * tall_one) for s in range(half)]
        return [(here[cut], there[cut]) for cut in cuts]

    def along(both, sums):
        return [*both[0], *[to_turn(value, s) for s, value in enumerate(sums, 1)]]

    def to_owner(terms):
        return send(summed(*terms).astype(bf16), lambda c, b, h, q: (c, 1 - b, 1 - h, q) if b != h else None)

    def chip_sum(part, here, there, *others):
        order = orders[part]
        there = to_chip(there, order[0])
        held = {}
        for n, r in enumerate(r for r in every if not r & order[0]):
            cut = slice(n * tall_two, (n + 1) * tall_two)
            held[r] = [here[cut], there[cut]]
        for bit in order[1:]:
            for r in [r for r in sorted(held) if r & bit]:
                held[r ^ bit].append(to_chip(after(summed(*held.pop(r)).astype(bf16), *others), bit))
        return held[0]

    def half_sum(parts, firsts, *others):
        fars = [
            send(
                after(summed(*terms).astype(bf16), first),
                lambda c, b, h, q: (c, b, 1 - h, q) if b != h else None,
            )
            for terms, first in zip(parts, firsts)
        ]
        sums = []
        for terms, far in zip(parts, fars):
            total = summed(*terms, far)
            up, down = total[: tall_two // 2], total[tall_two // 2 :]
            passed = send(
                after(jnp.where(core == 0, down, up).astype(bf16), *others),
                lambda c, b, h, q: (c, 1 - b, h, q) if b == h else None,
            )
            sums.append(jnp.where(home, jnp.where(core == 0, up, down), passed.astype(f32)))
        return sums

    def outer(module, moment, sums):
        average = jnp.concatenate(sums, axis=1)[None]
        following = outer_moment * moment + average
        return module - outer_rate * (outer_moment * following + average), following

    there_a, there_b = deltas(calls[0])
    here_a, here_b = deltas(calls[1], there_a)
    both_a, both_b = both_cores(here_a, there_a), both_cores(here_b, there_b)
    sums_a, sums_b = ([summed(*pair).astype(bf16) for pair in both[1:]] for both in (both_a, both_b))
    leave_a, leave_b = deltas(calls[2], here_a, *sums_a, *sums_b)
    along_a, along_b = along(both_a, sums_a), along(both_b, sums_b)
    stay_a, stay_b = deltas(calls[3], leave_a, along_a[-1])
    owned_a, owned_b = to_owner(along_a), to_owner(along_b)
    sums_one = [
        jnp.where(home, summed(*terms), owned.astype(f32))
        for terms, owned in ((along_a, owned_a), (along_b, owned_b))
    ]
    new_one, next_moment_one = outer(module_one, moment_one, sums_one)
    chip_a = chip_sum(0, stay_a, leave_a, owned_a)
    chip_b = chip_sum(1, stay_b, leave_b, owned_a)
    sums_two = half_sum((chip_a, chip_b), (owned_b, owned_b), new_one, next_moment_one)
    new_two, next_moment_two = outer(module_two, moment_two, sums_two)
    return (new_one, new_two, next_moment_one, next_moment_two)


def solution(mesh):
    return jax.shard_map(
        shards,
        mesh=mesh,
        in_specs=(
            P(None, ("row", "col"), None),
            P(None, ("row", "col"), None),
            P(None, ("row", "col"), None),
            P(),
            P("row", "col", None),
            P("col", "row", None),
            P("row", "col", None),
            P("col", "row", None),
        ),
        out_specs=(
            P("row", "col", None),
            P("col", "row", None),
            P("row", "col", None),
            P("col", "row", None),
        ),
        check_vma=False,
    )
```

```python
import functools

import jax
import jax.numpy as jnp
from jax import lax
from jax.experimental import pallas as pl
from jax.experimental.pallas import tpu as pltpu
from jax.sharding import PartitionSpec as P

beta_one = 0.9
beta_two = 0.95
inner_rate = 0.1
decay = 0.1
outer_rate = 0.7
outer_moment = 0.9

VMEM_LIMIT = 56 * 1024 * 1024
f32 = jnp.float32
bf16 = jnp.bfloat16


def step_kernel(rows_dev, tile, keep, base, one_at, two_at, *refs):
    n_one, n_two = len(one_at), len(two_at)
    place_ref, xy_ref = refs[:2]
    refs = refs[2:]

    def take(places):
        nonlocal refs
        found = [tuple(refs[sum(p[1] for p in places[:i]) :][: p[1]]) for i, p in enumerate(places)]
        refs = refs[sum(p[1] for p in places) :]
        return found

    one_refs, two_refs = take(one_at), take(two_at)
    left_ref, right_ref = refs[:2]
    start_out = refs[2] if keep else None
    one, two, pre, one_sem, two_sem, out_sem = refs[-6:]
    width = one.shape[0]
    scale = width ** (-0.5)
    parts = width // tile
    home = place_ref[base + n_one + n_two]

    class Copies:
        def __init__(self, *choices):
            self.choices = choices

        def start(self):
            if len(self.choices) == 1:
                self.choices[0].start()
            else:
                pl.when(home == 1)(self.choices[0].start)
                pl.when(home == 0)(self.choices[1].start)

        def wait(self):
            self.choices[0].wait()

    def one_copies(n):
        found = []
        for i, (pieces, (first, _, top, tall)) in enumerate(zip(one_refs, one_at)):
            wide = pieces[0].shape[1]
            if first <= n * tile < first + wide:
                down = pl.ds(pl.multiple_of(place_ref[base + i] * tall, tall), tall)
                found.append(
                    Copies(*[
                        pltpu.make_async_copy(
                            piece.at[pl.ds(top, tall), pl.ds(n * tile - first, tile)],
                            one.at[down, pl.ds(n * tile, tile)],
                            one_sem.at[i, n],
                        )
                        for piece in pieces
                    ])
                )
        return found

    two_copies = []
    for i, (pieces, (first, _, top, tall)) in enumerate(zip(two_refs, two_at)):
        wide = pieces[0].shape[1]
        down = pl.ds(pl.multiple_of(place_ref[base + n_one + i] * tall, tall), tall)
        two_copies.append(
            Copies(*[
                pltpu.make_async_copy(piece.at[pl.ds(top, tall), :], two.at[down, pl.ds(first, wide)], two_sem.at[i])
                for piece in pieces
            ])
        )
    for n in range(parts):
        for copy in one_copies(n):
            copy.start()
    for copy in two_copies:
        copy.start()
    for n in range(parts):
        span = pl.ds(n * tile, tile)
        for copy in one_copies(n):
            copy.wait()
        value = jnp.dot(xy_ref[:, :width], one[:, span], preferred_element_type=f32) * scale
        pre[:, span] = value
        left_ref[:, span] = xy_ref[:, span]
        left_ref[:, pl.ds(width + n * tile, tile)] = (value * jax.nn.sigmoid(value)).astype(bf16)
    for copy in two_copies:
        copy.wait()
    if keep:
        one_save = pltpu.make_async_copy(one, start_out.at[pl.ds(0, width), :], out_sem.at[0])
        two_save = pltpu.make_async_copy(two, start_out.at[pl.ds(width, width), :], out_sem.at[1])
        one_save.start()
        two_save.start()

    def miss(n, carry):
        span = pl.ds(pl.multiple_of(n * tile, tile), tile)
        late = pl.ds(pl.multiple_of(width + n * tile, tile), tile)
        out = xy_ref[:, span].astype(f32) + jnp.dot(left_ref[:, width:], two[:, span], preferred_element_type=f32) * scale
        right_ref[:, late] = ((out - xy_ref[:, late].astype(f32)) / rows_dev).astype(bf16)
        return carry

    lax.fori_loop(0, parts, miss, 0)

    def backward(n, carry):
        span = pl.ds(pl.multiple_of(n * tile, tile), tile)
        back = lax.dot_general(
            right_ref[:, width:], two[span, :], (((1,), (1,)), ((), ())), preferred_element_type=f32
        ) * scale
        value = pre[:, span]
        sig = jax.nn.sigmoid(value)
        right_ref[:, span] = (back * (sig * (1.0 + value * (1.0 - sig)))).astype(bf16)
        return carry

    lax.fori_loop(0, parts, backward, 0)
    if keep:
        one_save.wait()
        two_save.wait()


def step(xy, one, two, rows_dev, keep, places, base):
    rows, width = xy.shape[0], xy.shape[1] // 2
    tile = 512
    vmem = pl.BlockSpec(memory_space=pltpu.VMEM)
    hbm = pl.BlockSpec(memory_space=pl.ANY)
    out = jax.ShapeDtypeStruct((rows, 2 * width), bf16)
    whole = jax.ShapeDtypeStruct((2 * width, width), bf16)
    sources = [array for p in one + two for array in p[0]]

    def entries(pieces):
        return tuple((p[1], len(p[0]), *(p[2:] or (0, p[0][0].shape[0]))) for p in pieces)

    return pl.pallas_call(
        functools.partial(
            step_kernel, rows_dev, tile, keep, base, entries(one), entries(two)
        ),
        out_shape=(out, out) + ((whole,) if keep else ()),
        in_specs=[pl.BlockSpec(memory_space=pltpu.SMEM), vmem] + [hbm] * len(sources),
        out_specs=(vmem, vmem) + ((hbm,) if keep else ()),
        scratch_shapes=[
            pltpu.VMEM((width, width), bf16),
            pltpu.VMEM((width, width), bf16),
            pltpu.VMEM((rows, width), f32),
            pltpu.SemaphoreType.DMA((len(one), width // tile)),
            pltpu.SemaphoreType.DMA((len(two),)),
            pltpu.SemaphoreType.DMA((2,)),
        ],
        compiler_params=pltpu.CompilerParams(vmem_limit_bytes=VMEM_LIMIT),
        cost_estimate=pl.CostEstimate(flops=15 * rows * width * width, bytes_accessed=4 * width * width, transcendentals=0),
    )(places, xy, *sources)


def update_kernel(guard, tile, a_ref, b_ref, p_ref, out_ref):
    shrink = inner_rate * decay
    turned = a_ref[...].T
    for n in range(p_ref.shape[1] // tile):
        span = slice(n * tile, (n + 1) * tile)
        grad = jnp.dot(turned, b_ref[:, span], preferred_element_type=f32)
        move = grad * pl.reciprocal(jnp.abs(grad) + guard, approx=True)
        out_ref[:, span] = (p_ref[:, span].astype(f32) * (1.0 - shrink) - inner_rate * move).astype(bf16)


def update(left, right, start, guard):
    rows, width = left.shape[0], start.shape[1]
    tall = 512
    each = width // tall
    return pl.pallas_call(
        functools.partial(update_kernel, guard * width ** 0.5, 512),
        out_shape=jax.ShapeDtypeStruct(start.shape, bf16),
        grid=(2 * each,),
        in_specs=[
            pl.BlockSpec((rows, tall), lambda m: (0, m)),
            pl.BlockSpec((rows, width), lambda m: (0, m // each)),
            pl.BlockSpec((tall, width), lambda m: (m, 0)),
        ],
        out_specs=pl.BlockSpec((tall, width), lambda m: (m, 0)),
        compiler_params=pltpu.CompilerParams(vmem_limit_bytes=VMEM_LIMIT),
        cost_estimate=pl.CostEstimate(flops=12 * rows * width * start.shape[0], bytes_accessed=4 * start.size, transcendentals=0),
    )(left, right, start)


def term_kernel(guard, tile, base, spans, place_ref, weight_ref, a_ref, b_ref, c_ref, d_ref, p_ref, *refs):
    outs, held, sem = refs[:-2], refs[-2], refs[-1]
    step = pl.program_id(0)
    slot = step % 2
    last = spans[-1][1]
    short, wide = p_ref.shape

    def copies(m, slot):
        return [
            (
                (m >= begin) & (m < end),
                pltpu.make_async_copy(
                    held.at[slot], out.at[pl.ds(pl.multiple_of((m - begin) * short, short), short), :], sem.at[slot]
                ),
            )
            for out, (begin, end) in zip(outs, spans)
        ]

    def settle(slot):
        pltpu.make_async_copy(held.at[slot], outs[0].at[pl.ds(0, short), :], sem.at[slot]).wait()

    @pl.when(step >= 2)
    def _():
        settle(slot)

    weight = jnp.where(place_ref[base + 3 * last + step] == 0, weight_ref[0], weight_ref[1])
    shrink = inner_rate * decay
    new_m = (1.0 - beta_one) / (1.0 - beta_one ** 2)
    new_v = ((1.0 - beta_two) / (1.0 - beta_two ** 2)) ** 0.5
    by_first = weight * (inner_rate * (1.0 - shrink))
    by_second = weight * (inner_rate * new_m / new_v)
    by_start = weight * (shrink * (2.0 - shrink))
    older, newer = a_ref[...].T, c_ref[...].T
    for n in range(wide // tile):
        span = slice(n * tile, (n + 1) * tile)
        old = jnp.dot(older, b_ref[:, span], preferred_element_type=f32)
        new = jnp.dot(newer, d_ref[:, span], preferred_element_type=f32)
        first = old * pl.reciprocal(jnp.abs(old) + guard, approx=True)
        square = beta_two * (old * old) + new * new
        root = square * lax.rsqrt(square + 1e-30)
        second = (beta_one * old + new) * pl.reciprocal(root + guard / new_v, approx=True)
        start = p_ref[:, span].astype(f32)
        held[slot, :, span] = (first * by_first + second * by_second + start * by_start).astype(bf16)
    for here, copy in copies(step, slot):
        pl.when(here)(copy.start)

    @pl.when(step == last - 1)
    def _():
        settle(slot)
        if last > 1:
            settle(1 - slot)


def terms(weights, places, base, counts, short, parts, a, b, c, d, p, guard):
    rows, width = a.shape[0], p.shape[1]
    wide = width // parts
    ends = [sum(counts[: n + 1]) for n in range(len(counts))]
    spans = tuple((end - count, end) for count, end in zip(counts, ends))
    last = ends[-1]
    row = lambda m, at: at[base + m]
    col = lambda m, at: at[base + last + m]
    both = lambda m, at: at[base + 2 * last + m]
    side = pl.BlockSpec((rows, short), lambda m, at: (0, row(m, at)))
    full = pl.BlockSpec((rows, wide), lambda m, at: (0, both(m, at)))
    return pl.pallas_call(
        functools.partial(term_kernel, guard * width ** 0.5, 256, base, spans),
        out_shape=tuple(jax.ShapeDtypeStruct((count * short, wide), bf16) for count in counts),
        grid_spec=pltpu.PrefetchScalarGridSpec(
            num_scalar_prefetch=1,
            grid=(last,),
            in_specs=[
                pl.BlockSpec(memory_space=pltpu.SMEM),
                side, full, side, full,
                pl.BlockSpec((short, wide), lambda m, at: (row(m, at), col(m, at))),
            ],
            out_specs=tuple(pl.BlockSpec(memory_space=pl.ANY) for _ in counts),
            scratch_shapes=[pltpu.VMEM((2, short, wide), bf16), pltpu.SemaphoreType.DMA((2,))],
        ),
        compiler_params=pltpu.CompilerParams(vmem_limit_bytes=VMEM_LIMIT),
        cost_estimate=pl.CostEstimate(flops=1, bytes_accessed=1, transcendentals=0),
    )(places, weights, a, b, c, d, p)


def slots(routes, documents, targets, device_of, room):
    dest = device_of(routes[:, 0])
    paths = device_of(None)
    hit = (dest[:, None] == jnp.arange(paths, dtype=jnp.int32)[None, :]).astype(jnp.int32)
    before = jnp.cumsum(hit, axis=0) - hit
    slot = dest * room + jnp.sum(before * hit, axis=1)
    place = (slot[:, None] == jnp.arange(paths * room, dtype=jnp.int32)[None, :]).astype(bf16)
    both = jnp.concatenate([documents, targets], axis=1)
    return jnp.einsum("rs,rd->sd", place, both, preferred_element_type=f32).astype(bf16)


def after(value, *others):
    return lax.optimization_barrier((value,) + others)[0]


def shards(documents, targets, routes, doc_counts, module_one, module_two, moment_one, moment_two):
    n_row = lax.axis_size("row")
    n_col = lax.axis_size("col")
    chips, half = n_row // 2, n_col // 2
    paths = n_row * n_col
    row_id = lax.axis_index("row")
    col_id = lax.axis_index("col")
    chip, core = row_id // 2, row_id % 2
    side, turn = col_id // half, col_id % half
    home = core == side
    micro, rows_dev, width = documents.shape
    room = max(2, 2 * rows_dev // paths)
    guard = 0.5 / (width * rows_dev) ** 0.5

    def device_of(path):
        if path is None:
            return paths
        i, j = path // n_col, path % n_col
        return (2 * (i // 2) + j // half) * n_col + (i % 2) * half + j % half

    def send(value, target):
        pairs = []
        for i in range(n_row):
            for k in range(n_col):
                to = target(i // 2, i % 2, k // half, k % half)
                if to is not None:
                    c, b, h, q = to
                    pairs.append((i * n_col + k, (2 * c + b) * n_col + h * half + q))
        return lax.ppermute(value, ("row", "col"), pairs)

    def to_core(value):
        return send(value, lambda c, b, h, q: (c, 1 - b, h, q))

    def to_turn(value, s):
        return send(value, lambda c, b, h, q: (c, b, h, (q + s) % half))

    def to_chip(value, bit):
        return send(value, lambda c, b, h, q: (c ^ bit, b, h, q))

    bits = [1 << t for t in range(chips.bit_length() - 1)]
    orders = [bits, bits[::-1]]
    cols = width // 2

    every = list(range(chips))
    tall_one, tall_two = width // n_col, width // chips
    short = min(tall_one, tall_two, 512)
    table = []

    def enter(*pieces):
        talls = (tall_one, tall_two)
        listed = [
            (
                level * (width // short) + block * (talls[level] // short) + cut,
                part,
                level * 2 + part,
                level,
            )
            for level, blocks, part in pieces
            for block in blocks
            for cut in range(talls[level] // short)
        ]
        base = len(table)
        for field in zip(*listed):
            table.extend(field)
        return base, tuple(len(blocks) * (talls[level] // short) for level, blocks, part in pieces)

    here = [(turn + s) % half + core * half for s in range(half)]
    there = [(turn + s) % half + (1 - core) * half for s in range(half)]
    leave = [[chip ^ r for r in every if r & order[0]] for order in orders]
    stay = [[chip ^ r for r in every if not r & order[0]] for order in orders]
    calls = [
        enter((0, there, 0), (0, there, 1)),
        enter((0, here, 0), (0, here, 1)),
        enter((1, leave[0], 0), (1, leave[1], 1)),
        enter((1, stay[0], 0), (1, stay[1], 1)),
    ]
    base_first = len(table)
    for part in range(2):
        for other in (core, 1 - core):
            table += [(turn - s) % half + other * half for s in range(half)]
    for order in orders:
        held = [0]
        for bit in order:
            held = held + [r ^ bit for r in held]
        table += [chip ^ r for r in held]
    table.append(home)
    base_second = len(table)
    table += [0, 0, 0]
    places = jnp.stack([jnp.asarray(value).astype(jnp.int32) for value in table])

    counts = doc_counts.astype(f32)
    path_one, path_two = 2 * chip + side, turn + core * half
    in_row = (jnp.arange(n_row) == path_one)[:, None]
    in_col = (jnp.arange(n_col) == path_two)[None, :]
    row_counts = jnp.sum(jnp.where(in_row, counts, 0.0))
    col_counts = jnp.sum(jnp.where(in_col, counts, 0.0))
    own_count = jnp.sum(jnp.where(in_row & in_col, counts, 0.0))
    weights = jnp.stack([own_count / row_counts, own_count / col_counts])

    sent = [slots(routes[s], documents[s], targets[s], device_of, room) for s in range(micro)]

    def exchange(value):
        return lax.all_to_all(
            value.reshape(paths, room, 2 * width), ("row", "col"), split_axis=0, concat_axis=0, tiled=True
        ).reshape(paths * room, 2 * width)

    own_two = module_two[0].astype(bf16)
    own_one = module_one[0].astype(bf16)
    other_two = send(own_two, lambda c, b, h, q: (c, h, h, q) if b != h else None)
    pair_two = jnp.where(
        core == 0,
        jnp.concatenate([own_two, other_two], axis=0),
        jnp.concatenate([other_two, own_two], axis=0),
    )

    def to_chips(value, bit, here):
        return send(value, lambda c, b, h, q: (c ^ bit, b, h, q) if (b == h) == here else None)

    def to_half(value, here):
        if half == 1:
            return jnp.zeros_like(value)
        return send(value, lambda c, b, h, q: (c, b, h, (q + 1) % half) if (b == h) == here else None)

    def begin(pair, here):
        own = [pair[:, part * cols : (part + 1) * cols] for part in range(2)]
        return [(value, to_chips(value, order[0], here)) for value, order in zip(own, orders)]

    def proceed(held, here):
        for n in range(1, len(bits)):
            held = [jnp.concatenate(pieces, axis=0) for pieces in held]
            held = [(value, to_chips(value, order[n], here)) for value, order in zip(held, orders)]
        return held

    def barrier(*values):
        return jax.tree.unflatten(jax.tree.structure(values), lax.optimization_barrier(jax.tree.leaves(values)))

    ones = [own_one[:, :cols], own_one[:, cols:]]

    def far_half(value):
        return send(value, lambda c, b, h, q: (c, 1 - b, 1 - h, q) if b != h else None)

    fars, nears = [far_half(ones[0])], [to_half(ones[0], True)]
    home_two = begin(pair_two, True)
    ones, fars, nears, pair_two, places, weights, sent = barrier(
        ones, fars, nears, pair_two, places, weights, sent
    )
    far_two = send(pair_two, lambda c, b, h, q: (c, b, 1 - h, q) if b == h else None)
    turns = [to_half(fars[0], False)]
    home_two = proceed(home_two, True)
    ones, fars, nears, turns, far_two, home_two, sent = barrier(ones, fars, nears, turns, far_two, home_two, sent)
    fars.append(far_half(ones[1]))
    nears.append(to_half(ones[1], True))
    away_two = begin(far_two, False)
    fars, nears, away_two, sent = barrier(fars, nears, away_two, sent)
    got_a = exchange(sent[0])
    turns.append(to_half(fars[1], False))
    away_two = proceed(away_two, False)
    one = []
    for part in range(2):
        held = [jnp.where(home, ones[part], fars[part])]
        if half > 1:
            held.append(jnp.where(home, nears[part], turns[part]))
        held += [to_turn(held[0], s) for s in range(2, half)]
        joined = jnp.concatenate(held, axis=0)
        for value in (joined, to_core(joined)):
            one += [((value,), part * cols, s * tall_one, tall_one) for s in range(half)]
    two = []
    for part in range(2):
        for mine, theirs in zip(home_two[part], away_two[part]):
            count = mine.shape[0] // tall_two
            two += [((mine, theirs), part * cols, n * tall_two, tall_two) for n in range(count)]
    got_b = exchange(after(sent[1], got_a, away_two[0][1], away_two[1][1]))
    left_a, right_a, start = step(got_a, one, two, rows_dev, True, places, base_first)
    moved = update(left_a, right_a, start, guard)
    left_b, right_b = step(got_b, [((moved,), 0, 0, width)], [((moved,), 0, width, width)], rows_dev, False, places, base_second)

    def deltas(call, *others):
        return terms(after(weights, *others), places, *call, short, 2, left_a, right_a, left_b, right_b, start, guard)

    def summed(*values):
        return functools.reduce(lambda x, y: x + y, [value.astype(f32) for value in values])

    def both_cores(here, there):
        there = to_core(there)
        cuts = [slice(s * tall_one, (s + 1) * tall_one) for s in range(half)]
        return [(here[cut], there[cut]) for cut in cuts]

    def along(both, sums):
        return [*both[0], *[to_turn(value, s) for s, value in enumerate(sums, 1)]]

    def to_owner(terms, *others):
        return send(
            after(summed(*terms).astype(bf16), *others),
            lambda c, b, h, q: (c, 1 - b, 1 - h, q) if b != h else None,
        )

    def chip_sum(part, here, there):
        there = to_chip(there, orders[part][0])
        cuts = [slice(n * tall_two, (n + 1) * tall_two) for n in range(chips // 2)]
        left = [r for r in every if not r & orders[part][0]]
        return {r: [here[cut], there[cut]] for r, cut in zip(left, cuts)}

    def chip_rest(part, held, *others):
        held = {r: list(pieces) for r, pieces in held.items()}
        for bit in orders[part][1:]:
            for r in [r for r in sorted(held) if r & bit]:
                held[r ^ bit].append(to_chip(after(summed(*held.pop(r)).astype(bf16), *others), bit))
        return held[0]

    def half_sum(terms, *others):
        total = summed(*terms)
        up, down = total[: tall_two // 2], total[tall_two // 2 :]
        near = send(
            jnp.where(core == 0, down, up).astype(bf16),
            lambda c, b, h, q: (c, 1 - b, h, q) if b == h else None,
        )
        fars = [
            send(
                after(rows.astype(bf16), *others),
                lambda c, b, h, q, to=to: (c, to, 1 - h, q) if b != h else None,
            )
            for to, rows in enumerate((up, down))
        ]
        return jnp.where(home, jnp.where(core == 0, up, down), near.astype(f32)) + jnp.where(
            core == 0, *[far.astype(f32) for far in fars]
        )

    def outer(module, moment, sums):
        average = jnp.concatenate(sums, axis=1)[None]
        following = outer_moment * moment + average
        return module - outer_rate * (outer_moment * following + average), following

    there_a, there_b = deltas(calls[0])
    here_a, here_b = deltas(calls[1], there_a)
    both_a, both_b = both_cores(here_a, there_a), both_cores(here_b, there_b)
    sums_a, sums_b = ([summed(*pair).astype(bf16) for pair in both[1:]] for both in (both_a, both_b))
    leave_a, leave_b = deltas(calls[2], here_a, *sums_a, *sums_b)
    along_a, along_b = along(both_a, sums_a), along(both_b, sums_b)
    stay_a, stay_b = deltas(calls[3], leave_a, along_a[-1])
    owned_a = to_owner(along_a)
    owned_b = to_owner(along_b, stay_a)
    chip_a, chip_b = chip_sum(0, stay_a, leave_a), chip_sum(1, stay_b, leave_b)
    chip_a, chip_b = chip_rest(0, chip_a, owned_a), chip_rest(1, chip_b, owned_a)
    sums_one = [
        jnp.where(home, summed(*terms), owned.astype(f32))
        for terms, owned in ((along_a, owned_a), (along_b, owned_b))
    ]
    new_one, next_moment_one = outer(module_one, moment_one, sums_one)
    sums_two = [half_sum(terms, owned_b) for terms in (chip_a, chip_b)]
    new_two, next_moment_two = outer(module_two, moment_two, sums_two)
    return (new_one, new_two, next_moment_one, next_moment_two)


def solution(mesh):
    return jax.shard_map(
        shards,
        mesh=mesh,
        in_specs=(
            P(None, ("row", "col"), None),
            P(None, ("row", "col"), None),
            P(None, ("row", "col"), None),
            P(),
            P("row", "col", None),
            P("col", "row", None),
            P("row", "col", None),
            P("col", "row", None),
        ),
        out_specs=(
            P("row", "col", None),
            P("col", "row", None),
            P("row", "col", None),
            P("col", "row", None),
        ),
        check_vma=False,
    )
```

```python
import functools

import jax
import jax.numpy as jnp
from jax import lax
from jax.experimental import pallas as pl
from jax.experimental.pallas import tpu as pltpu
from jax.sharding import PartitionSpec as P

beta_one = 0.9
beta_two = 0.95
inner_rate = 0.1
decay = 0.1
outer_rate = 0.7
outer_moment = 0.9

VMEM_LIMIT = 32 * 1024 * 1024
f32 = jnp.float32
bf16 = jnp.bfloat16


def step_kernel(rows_dev, tile, keep, base, one_at, two_at, *refs):
    n_one, n_two = len(one_at), len(two_at)
    place_ref, xy_ref = refs[:2]
    refs = refs[2:]

    def take(places):
        nonlocal refs
        found = [tuple(refs[sum(p[1] for p in places[:i]) :][: p[1]]) for i, p in enumerate(places)]
        refs = refs[sum(p[1] for p in places) :]
        return found

    one_refs, two_refs = take(one_at), take(two_at)
    left_ref, right_ref = refs[:2]
    start_out = refs[2] if keep else None
    one, two, pre, one_sem, two_sem, out_sem = refs[-6:]
    width = one.shape[0]
    scale = width ** (-0.5)
    parts = width // tile
    home = place_ref[base + n_one + n_two]

    class Copies:
        def __init__(self, *choices):
            self.choices = choices

        def start(self):
            if len(self.choices) == 1:
                self.choices[0].start()
            else:
                pl.when(home == 1)(self.choices[0].start)
                pl.when(home == 0)(self.choices[1].start)

        def wait(self):
            self.choices[0].wait()

    def one_copies(n):
        found = []
        for i, (pieces, (first, _, top, tall)) in enumerate(zip(one_refs, one_at)):
            wide = pieces[0].shape[1]
            if first <= n * tile < first + wide:
                down = pl.ds(pl.multiple_of(place_ref[base + i] * tall, tall), tall)
                found.append(
                    Copies(*[
                        pltpu.make_async_copy(
                            piece.at[pl.ds(top, tall), pl.ds(n * tile - first, tile)],
                            one.at[down, pl.ds(n * tile, tile)],
                            one_sem.at[i, n],
                        )
                        for piece in pieces
                    ])
                )
        return found

    two_copies = []
    for i, (pieces, (first, _, top, tall)) in enumerate(zip(two_refs, two_at)):
        wide = pieces[0].shape[1]
        down = pl.ds(pl.multiple_of(place_ref[base + n_one + i] * tall, tall), tall)
        two_copies.append(
            Copies(*[
                pltpu.make_async_copy(piece.at[pl.ds(top, tall), :], two.at[down, pl.ds(first, wide)], two_sem.at[i])
                for piece in pieces
            ])
        )
    for n in range(parts):
        for copy in one_copies(n):
            copy.start()
    for copy in two_copies:
        copy.start()
    for n in range(parts):
        span = pl.ds(n * tile, tile)
        for copy in one_copies(n):
            copy.wait()
        value = jnp.dot(xy_ref[:, :width], one[:, span], preferred_element_type=f32) * scale
        pre[:, span] = value
        left_ref[:, span] = xy_ref[:, span]
        left_ref[:, pl.ds(width + n * tile, tile)] = (value * jax.nn.sigmoid(value)).astype(bf16)
    for copy in two_copies:
        copy.wait()
    if keep:
        one_save = pltpu.make_async_copy(one, start_out.at[pl.ds(0, width), :], out_sem.at[0])
        two_save = pltpu.make_async_copy(two, start_out.at[pl.ds(width, width), :], out_sem.at[1])
        one_save.start()
        two_save.start()

    def miss(n, carry):
        span = pl.ds(pl.multiple_of(n * tile, tile), tile)
        late = pl.ds(pl.multiple_of(width + n * tile, tile), tile)
        out = xy_ref[:, span].astype(f32) + jnp.dot(left_ref[:, width:], two[:, span], preferred_element_type=f32) * scale
        right_ref[:, late] = ((out - xy_ref[:, late].astype(f32)) / rows_dev).astype(bf16)
        return carry

    lax.fori_loop(0, parts, miss, 0)

    def backward(n, carry):
        span = pl.ds(pl.multiple_of(n * tile, tile), tile)
        back = lax.dot_general(
            right_ref[:, width:], two[span, :], (((1,), (1,)), ((), ())), preferred_element_type=f32
        ) * scale
        value = pre[:, span]
        sig = jax.nn.sigmoid(value)
        right_ref[:, span] = (back * (sig * (1.0 + value * (1.0 - sig)))).astype(bf16)
        return carry

    lax.fori_loop(0, parts, backward, 0)
    if keep:
        one_save.wait()
        two_save.wait()


def step(xy, one, two, rows_dev, keep, places, base):
    rows, width = xy.shape[0], xy.shape[1] // 2
    tile = 512
    vmem = pl.BlockSpec(memory_space=pltpu.VMEM)
    hbm = pl.BlockSpec(memory_space=pl.ANY)
    out = jax.ShapeDtypeStruct((rows, 2 * width), bf16)
    whole = jax.ShapeDtypeStruct((2 * width, width), bf16)
    sources = [array for p in one + two for array in p[0]]

    def entries(pieces):
        return tuple((p[1], len(p[0]), *(p[2:] or (0, p[0][0].shape[0]))) for p in pieces)

    return pl.pallas_call(
        functools.partial(
            step_kernel, rows_dev, tile, keep, base, entries(one), entries(two)
        ),
        out_shape=(out, out) + ((whole,) if keep else ()),
        in_specs=[pl.BlockSpec(memory_space=pltpu.SMEM), vmem] + [hbm] * len(sources),
        out_specs=(vmem, vmem) + ((hbm,) if keep else ()),
        scratch_shapes=[
            pltpu.VMEM((width, width), bf16),
            pltpu.VMEM((width, width), bf16),
            pltpu.VMEM((rows, width), f32),
            pltpu.SemaphoreType.DMA((len(one), width // tile)),
            pltpu.SemaphoreType.DMA((len(two),)),
            pltpu.SemaphoreType.DMA((2,)),
        ],
        compiler_params=pltpu.CompilerParams(vmem_limit_bytes=VMEM_LIMIT),
        cost_estimate=pl.CostEstimate(flops=15 * rows * width * width, bytes_accessed=4 * width * width, transcendentals=0),
    )(places, xy, *sources)


def update_kernel(guard, tile, a_ref, b_ref, p_ref, out_ref):
    shrink = inner_rate * decay
    turned = a_ref[...].T
    for n in range(p_ref.shape[1] // tile):
        span = slice(n * tile, (n + 1) * tile)
        grad = jnp.dot(turned, b_ref[:, span], preferred_element_type=f32)
        move = grad * pl.reciprocal(jnp.abs(grad) + guard, approx=True)
        out_ref[:, span] = (p_ref[:, span].astype(f32) * (1.0 - shrink) - inner_rate * move).astype(bf16)


def update(left, right, start, guard):
    rows, width = left.shape[0], start.shape[1]
    tall = 512
    each = width // tall
    return pl.pallas_call(
        functools.partial(update_kernel, guard * width ** 0.5, 512),
        out_shape=jax.ShapeDtypeStruct(start.shape, bf16),
        grid=(2 * each,),
        in_specs=[
            pl.BlockSpec((rows, tall), lambda m: (0, m)),
            pl.BlockSpec((rows, width), lambda m: (0, m // each)),
            pl.BlockSpec((tall, width), lambda m: (m, 0)),
        ],
        out_specs=pl.BlockSpec((tall, width), lambda m: (m, 0)),
        compiler_params=pltpu.CompilerParams(vmem_limit_bytes=VMEM_LIMIT),
        cost_estimate=pl.CostEstimate(flops=12 * rows * width * start.shape[0], bytes_accessed=4 * start.size, transcendentals=0),
    )(left, right, start)


def term_kernel(guard, tile, base, spans, place_ref, weight_ref, a_ref, b_ref, c_ref, d_ref, p_ref, *refs):
    outs, held, sem = refs[:-2], refs[-2], refs[-1]
    step = pl.program_id(0)
    slot = step % 2
    last = spans[-1][1]
    short, wide = p_ref.shape

    def copies(m, slot):
        return [
            (
                (m >= begin) & (m < end),
                pltpu.make_async_copy(
                    held.at[slot], out.at[pl.ds(pl.multiple_of((m - begin) * short, short), short), :], sem.at[slot]
                ),
            )
            for out, (begin, end) in zip(outs, spans)
        ]

    def settle(slot):
        pltpu.make_async_copy(held.at[slot], outs[0].at[pl.ds(0, short), :], sem.at[slot]).wait()

    @pl.when(step >= 2)
    def _():
        settle(slot)

    weight = jnp.where(place_ref[base + 3 * last + step] == 0, weight_ref[0], weight_ref[1])
    shrink = inner_rate * decay
    new_m = (1.0 - beta_one) / (1.0 - beta_one ** 2)
    new_v = ((1.0 - beta_two) / (1.0 - beta_two ** 2)) ** 0.5
    by_first = weight * (inner_rate * (1.0 - shrink))
    by_second = weight * (inner_rate * new_m / new_v)
    by_start = weight * (shrink * (2.0 - shrink))
    older, newer = a_ref[...].T, c_ref[...].T
    for n in range(wide // tile):
        span = slice(n * tile, (n + 1) * tile)
        old = jnp.dot(older, b_ref[:, span], preferred_element_type=f32)
        new = jnp.dot(newer, d_ref[:, span], preferred_element_type=f32)
        first = old * pl.reciprocal(jnp.abs(old) + guard, approx=True)
        square = beta_two * (old * old) + new * new
        root = square * lax.rsqrt(square + 1e-30)
        second = (beta_one * old + new) * pl.reciprocal(root + guard / new_v, approx=True)
        start = p_ref[:, span].astype(f32)
        held[slot, :, span] = (first * by_first + second * by_second + start * by_start).astype(bf16)
    for here, copy in copies(step, slot):
        pl.when(here)(copy.start)

    @pl.when(step == last - 1)
    def _():
        settle(slot)
        if last > 1:
            settle(1 - slot)


def terms(weights, places, base, counts, short, parts, a, b, c, d, p, guard):
    rows, width = a.shape[0], p.shape[1]
    wide = width // parts
    ends = [sum(counts[: n + 1]) for n in range(len(counts))]
    spans = tuple((end - count, end) for count, end in zip(counts, ends))
    last = ends[-1]
    row = lambda m, at: at[base + m]
    col = lambda m, at: at[base + last + m]
    both = lambda m, at: at[base + 2 * last + m]
    side = pl.BlockSpec((rows, short), lambda m, at: (0, row(m, at)))
    full = pl.BlockSpec((rows, wide), lambda m, at: (0, both(m, at)))
    return pl.pallas_call(
        functools.partial(term_kernel, guard * width ** 0.5, 256, base, spans),
        out_shape=tuple(jax.ShapeDtypeStruct((count * short, wide), bf16) for count in counts),
        grid_spec=pltpu.PrefetchScalarGridSpec(
            num_scalar_prefetch=1,
            grid=(last,),
            in_specs=[
                pl.BlockSpec(memory_space=pltpu.SMEM),
                side, full, side, full,
                pl.BlockSpec((short, wide), lambda m, at: (row(m, at), col(m, at))),
            ],
            out_specs=tuple(pl.BlockSpec(memory_space=pl.ANY) for _ in counts),
            scratch_shapes=[pltpu.VMEM((2, short, wide), bf16), pltpu.SemaphoreType.DMA((2,))],
        ),
        compiler_params=pltpu.CompilerParams(vmem_limit_bytes=VMEM_LIMIT),
        cost_estimate=pl.CostEstimate(flops=1, bytes_accessed=1, transcendentals=0),
    )(places, weights, a, b, c, d, p)


def slots(routes, documents, targets, device_of, room):
    dest = device_of(routes[:, 0])
    paths = device_of(None)
    hit = (dest[:, None] == jnp.arange(paths, dtype=jnp.int32)[None, :]).astype(jnp.int32)
    before = jnp.cumsum(hit, axis=0) - hit
    slot = dest * room + jnp.sum(before * hit, axis=1)
    place = (slot[:, None] == jnp.arange(paths * room, dtype=jnp.int32)[None, :]).astype(bf16)
    both = jnp.concatenate([documents, targets], axis=1)
    return jnp.einsum("rs,rd->sd", place, both, preferred_element_type=f32).astype(bf16)


def after(value, *others):
    return lax.optimization_barrier((value,) + others)[0]


def shards(documents, targets, routes, doc_counts, module_one, module_two, moment_one, moment_two):
    n_row = lax.axis_size("row")
    n_col = lax.axis_size("col")
    chips, half = n_row // 2, n_col // 2
    paths = n_row * n_col
    row_id = lax.axis_index("row")
    col_id = lax.axis_index("col")
    chip, core = row_id // 2, row_id % 2
    side, turn = col_id // half, col_id % half
    home = core == side
    micro, rows_dev, width = documents.shape
    room = max(2, 2 * rows_dev // paths)
    guard = 0.5 / (width * rows_dev) ** 0.5

    def device_of(path):
        if path is None:
            return paths
        i, j = path // n_col, path % n_col
        return (2 * (i // 2) + j // half) * n_col + (i % 2) * half + j % half

    def send(value, target):
        pairs = []
        for i in range(n_row):
            for k in range(n_col):
                to = target(i // 2, i % 2, k // half, k % half)
                if to is not None:
                    c, b, h, q = to
                    pairs.append((i * n_col + k, (2 * c + b) * n_col + h * half + q))
        return lax.ppermute(value, ("row", "col"), pairs)

    def to_core(value):
        return send(value, lambda c, b, h, q: (c, 1 - b, h, q))

    def to_turn(value, s):
        return send(value, lambda c, b, h, q: (c, b, h, (q + s) % half))

    def to_chip(value, bit):
        return send(value, lambda c, b, h, q: (c ^ bit, b, h, q))

    bits = [1 << t for t in range(chips.bit_length() - 1)]
    orders = [bits, bits[::-1]]
    cols = width // 2

    every = list(range(chips))
    tall_one, tall_two = width // n_col, width // chips
    short = min(tall_one, tall_two, 512)
    table = []

    def enter(*pieces):
        talls = (tall_one, tall_two)
        listed = [
            (
                level * (width // short) + block * (talls[level] // short) + cut,
                part,
                level * 2 + part,
                level,
            )
            for level, blocks, part in pieces
            for block in blocks
            for cut in range(talls[level] // short)
        ]
        base = len(table)
        for field in zip(*listed):
            table.extend(field)
        return base, tuple(len(blocks) * (talls[level] // short) for level, blocks, part in pieces)

    here = [(turn + s) % half + core * half for s in range(half)]
    there = [(turn + s) % half + (1 - core) * half for s in range(half)]
    leave = [[chip ^ r for r in every if r & order[0]] for order in orders]
    stay = [[chip ^ r for r in every if not r & order[0]] for order in orders]
    calls = [
        enter((0, there, 0), (0, there, 1)),
        enter((0, here, 0), (0, here, 1)),
        enter((1, leave[0], 0), (1, leave[1], 1)),
        enter((1, stay[0], 0), (1, stay[1], 1)),
    ]
    base_first = len(table)
    for part in range(2):
        for other in (core, 1 - core):
            table += [(turn - s) % half + other * half for s in range(half)]
    for order in orders:
        held = [0]
        for bit in order:
            held = held + [r ^ bit for r in held]
        table += [chip ^ r for r in held]
    table.append(home)
    base_second = len(table)
    table += [0, 0, 0]
    places = jnp.stack([jnp.asarray(value).astype(jnp.int32) for value in table])

    counts = doc_counts.astype(f32)
    path_one, path_two = 2 * chip + side, turn + core * half
    in_row = (jnp.arange(n_row) == path_one)[:, None]
    in_col = (jnp.arange(n_col) == path_two)[None, :]
    row_counts = jnp.sum(jnp.where(in_row, counts, 0.0))
    col_counts = jnp.sum(jnp.where(in_col, counts, 0.0))
    own_count = jnp.sum(jnp.where(in_row & in_col, counts, 0.0))
    weights = jnp.stack([own_count / row_counts, own_count / col_counts])

    sent = [slots(routes[s], documents[s], targets[s], device_of, room) for s in range(micro)]

    def exchange(value):
        return lax.all_to_all(
            value.reshape(paths, room, 2 * width), ("row", "col"), split_axis=0, concat_axis=0, tiled=True
        ).reshape(paths * room, 2 * width)

    own_two = module_two[0].astype(bf16)
    own_one = module_one[0].astype(bf16)
    other_two = send(own_two, lambda c, b, h, q: (c, h, h, q) if b != h else None)
    pair_two = jnp.where(
        core == 0,
        jnp.concatenate([own_two, other_two], axis=0),
        jnp.concatenate([other_two, own_two], axis=0),
    )

    def to_chips(value, bit, here):
        return send(value, lambda c, b, h, q: (c ^ bit, b, h, q) if (b == h) == here else None)

    def to_half(value, here):
        if half == 1:
            return jnp.zeros_like(value)
        return send(value, lambda c, b, h, q: (c, b, h, (q + 1) % half) if (b == h) == here else None)

    def begin(pair, here):
        own = [pair[:, part * cols : (part + 1) * cols] for part in range(2)]
        return [(value, to_chips(value, order[0], here)) for value, order in zip(own, orders)]

    def proceed(held, here):
        for n in range(1, len(bits)):
            held = [jnp.concatenate(pieces, axis=0) for pieces in held]
            held = [(value, to_chips(value, order[n], here)) for value, order in zip(held, orders)]
        return held

    def barrier(*values):
        return jax.tree.unflatten(jax.tree.structure(values), lax.optimization_barrier(jax.tree.leaves(values)))

    ones = [own_one[:, :cols], own_one[:, cols:]]

    def far_half(value):
        return send(value, lambda c, b, h, q: (c, 1 - b, 1 - h, q) if b != h else None)

    fars, nears = [far_half(ones[0])], [to_half(ones[0], True)]
    home_two = begin(pair_two, True)
    ones, fars, nears, pair_two, places, weights, sent = barrier(
        ones, fars, nears, pair_two, places, weights, sent
    )
    far_two = send(pair_two, lambda c, b, h, q: (c, b, 1 - h, q) if b == h else None)
    turns = [to_half(fars[0], False)]
    home_two = proceed(home_two, True)
    ones, fars, nears, turns, far_two, home_two, sent = barrier(ones, fars, nears, turns, far_two, home_two, sent)
    fars.append(far_half(ones[1]))
    nears.append(to_half(ones[1], True))
    away_two = begin(far_two, False)
    fars, nears, away_two, sent = barrier(fars, nears, away_two, sent)
    got_a = exchange(sent[0])
    turns.append(to_half(fars[1], False))
    away_two = proceed(away_two, False)
    one = []
    for part in range(2):
        held = [jnp.where(home, ones[part], fars[part])]
        if half > 1:
            held.append(jnp.where(home, nears[part], turns[part]))
        held += [to_turn(held[0], s) for s in range(2, half)]
        joined = jnp.concatenate(held, axis=0)
        for value in (joined, to_core(joined)):
            one += [((value,), part * cols, s * tall_one, tall_one) for s in range(half)]
    two = []
    for part in range(2):
        for mine, theirs in zip(home_two[part], away_two[part]):
            count = mine.shape[0] // tall_two
            two += [((mine, theirs), part * cols, n * tall_two, tall_two) for n in range(count)]
    got_b = exchange(after(sent[1], got_a, away_two[0][1], away_two[1][1]))
    left_a, right_a, start = step(got_a, one, two, rows_dev, True, places, base_first)
    moved = update(left_a, right_a, start, guard)
    left_b, right_b = step(got_b, [((moved,), 0, 0, width)], [((moved,), 0, width, width)], rows_dev, False, places, base_second)

    def deltas(call, *others):
        return terms(after(weights, *others), places, *call, short, 2, left_a, right_a, left_b, right_b, start, guard)

    def summed(*values):
        return functools.reduce(lambda x, y: x + y, [value.astype(f32) for value in values])

    def both_cores(here, there):
        there = to_core(there)
        cuts = [slice(s * tall_one, (s + 1) * tall_one) for s in range(half)]
        return [(here[cut], there[cut]) for cut in cuts]

    def along(both, sums):
        return [*both[0], *[to_turn(value, s) for s, value in enumerate(sums, 1)]]

    def to_owner(terms, *others):
        return send(
            after(summed(*terms).astype(bf16), *others),
            lambda c, b, h, q: (c, 1 - b, 1 - h, q) if b != h else None,
        )

    def chip_sum(part, here, there):
        there = to_chip(there, orders[part][0])
        cuts = [slice(n * tall_two, (n + 1) * tall_two) for n in range(chips // 2)]
        left = [r for r in every if not r & orders[part][0]]
        return {r: [here[cut], there[cut]] for r, cut in zip(left, cuts)}

    def chip_rest(part, held, *others):
        held = {r: list(pieces) for r, pieces in held.items()}
        for bit in orders[part][1:]:
            for r in [r for r in sorted(held) if r & bit]:
                held[r ^ bit].append(to_chip(after(summed(*held.pop(r)).astype(bf16), *others), bit))
        return held[0]

    def half_sum(terms, *others):
        total = summed(*terms)
        up, down = total[: tall_two // 2], total[tall_two // 2 :]
        near = send(
            jnp.where(core == 0, down, up).astype(bf16),
            lambda c, b, h, q: (c, 1 - b, h, q) if b == h else None,
        )
        fars = [
            send(
                after(rows.astype(bf16), *others),
                lambda c, b, h, q, to=to: (c, to, 1 - h, q) if b != h else None,
            )
            for to, rows in enumerate((up, down))
        ]
        return jnp.where(home, jnp.where(core == 0, up, down), near.astype(f32)) + jnp.where(
            core == 0, *[far.astype(f32) for far in fars]
        )

    def outer(module, moment, sums):
        average = jnp.concatenate(sums, axis=1)[None]
        following = outer_moment * moment + average
        return module - outer_rate * (outer_moment * following + average), following

    there_a, there_b = deltas(calls[0])
    here_a, here_b = deltas(calls[1], there_a)
    both_a, both_b = both_cores(here_a, there_a), both_cores(here_b, there_b)
    sums_a, sums_b = ([summed(*pair).astype(bf16) for pair in both[1:]] for both in (both_a, both_b))
    leave_a, leave_b = deltas(calls[2], here_a, *sums_a, *sums_b)
    along_a, along_b = along(both_a, sums_a), along(both_b, sums_b)
    stay_a, stay_b = deltas(calls[3], leave_a, along_a[-1])
    owned_a = to_owner(along_a)
    owned_b = to_owner(along_b, stay_a)
    chip_a, chip_b = chip_sum(0, stay_a, leave_a), chip_sum(1, stay_b, leave_b)
    chip_a, chip_b = chip_rest(0, chip_a, owned_a), chip_rest(1, chip_b, owned_a)
    sums_one = [
        jnp.where(home, summed(*terms), owned.astype(f32))
        for terms, owned in ((along_a, owned_a), (along_b, owned_b))
    ]
    new_one, next_moment_one = outer(module_one, moment_one, sums_one)
    sums_two = [half_sum(terms, owned_b) for terms in (chip_a, chip_b)]
    new_two, next_moment_two = outer(module_two, moment_two, sums_two)
    return (new_one, new_two, next_moment_one, next_moment_two)


def solution(mesh):
    return jax.shard_map(
        shards,
        mesh=mesh,
        in_specs=(
            P(None, ("row", "col"), None),
            P(None, ("row", "col"), None),
            P(None, ("row", "col"), None),
            P(),
            P("row", "col", None),
            P("col", "row", None),
            P("row", "col", None),
            P("col", "row", None),
        ),
        out_specs=(
            P("row", "col", None),
            P("col", "row", None),
            P("row", "col", None),
            P("col", "row", None),
        ),
        check_vma=False,
    )
```

```python
import functools

import jax
import jax.numpy as jnp
from jax import lax
from jax.experimental import pallas as pl
from jax.experimental.pallas import tpu as pltpu
from jax.sharding import PartitionSpec as P

beta_one = 0.9
beta_two = 0.95
inner_rate = 0.1
decay = 0.1
outer_rate = 0.7
outer_moment = 0.9

STEP_VMEM = 56 * 1024 * 1024
TILE_VMEM = 32 * 1024 * 1024
f32 = jnp.float32
bf16 = jnp.bfloat16


def step_kernel(rows_dev, tile, keep, base, one_at, two_at, *refs):
    n_one, n_two = len(one_at), len(two_at)
    place_ref, xy_ref = refs[:2]
    refs = refs[2:]

    def take(places):
        nonlocal refs
        found = [tuple(refs[sum(p[1] for p in places[:i]) :][: p[1]]) for i, p in enumerate(places)]
        refs = refs[sum(p[1] for p in places) :]
        return found

    one_refs, two_refs = take(one_at), take(two_at)
    left_ref, right_ref = refs[:2]
    start_out = refs[2] if keep else None
    one, two, pre, one_sem, two_sem, out_sem = refs[-6:]
    width = one.shape[0]
    scale = width ** (-0.5)
    parts = width // tile
    home = place_ref[base + n_one + n_two]

    class Copies:
        def __init__(self, *choices):
            self.choices = choices

        def start(self):
            if len(self.choices) == 1:
                self.choices[0].start()
            else:
                pl.when(home == 1)(self.choices[0].start)
                pl.when(home == 0)(self.choices[1].start)

        def wait(self):
            self.choices[0].wait()

    def one_copies(n):
        found = []
        for i, (pieces, (first, _, top, tall)) in enumerate(zip(one_refs, one_at)):
            wide = pieces[0].shape[1]
            if first <= n * tile < first + wide:
                down = pl.ds(pl.multiple_of(place_ref[base + i] * tall, tall), tall)
                found.append(
                    Copies(*[
                        pltpu.make_async_copy(
                            piece.at[pl.ds(top, tall), pl.ds(n * tile - first, tile)],
                            one.at[down, pl.ds(n * tile, tile)],
                            one_sem.at[i, n],
                        )
                        for piece in pieces
                    ])
                )
        return found

    two_copies = []
    for i, (pieces, (first, _, top, tall)) in enumerate(zip(two_refs, two_at)):
        wide = pieces[0].shape[1]
        down = pl.ds(pl.multiple_of(place_ref[base + n_one + i] * tall, tall), tall)
        two_copies.append(
            Copies(*[
                pltpu.make_async_copy(piece.at[pl.ds(top, tall), :], two.at[down, pl.ds(first, wide)], two_sem.at[i])
                for piece in pieces
            ])
        )
    for n in range(parts):
        for copy in one_copies(n):
            copy.start()
    for copy in two_copies:
        copy.start()
    for n in range(parts):
        span = pl.ds(n * tile, tile)
        for copy in one_copies(n):
            copy.wait()
        value = jnp.dot(xy_ref[:, :width], one[:, span], preferred_element_type=f32) * scale
        pre[:, span] = value
        left_ref[:, span] = xy_ref[:, span]
        left_ref[:, pl.ds(width + n * tile, tile)] = (value * jax.nn.sigmoid(value)).astype(bf16)
    for copy in two_copies:
        copy.wait()
    if keep:
        one_save = pltpu.make_async_copy(one, start_out.at[pl.ds(0, width), :], out_sem.at[0])
        two_save = pltpu.make_async_copy(two, start_out.at[pl.ds(width, width), :], out_sem.at[1])
        one_save.start()
        two_save.start()

    def miss(n, carry):
        span = pl.ds(pl.multiple_of(n * tile, tile), tile)
        late = pl.ds(pl.multiple_of(width + n * tile, tile), tile)
        out = xy_ref[:, span].astype(f32) + jnp.dot(left_ref[:, width:], two[:, span], preferred_element_type=f32) * scale
        right_ref[:, late] = ((out - xy_ref[:, late].astype(f32)) / rows_dev).astype(bf16)
        return carry

    lax.fori_loop(0, parts, miss, 0, unroll=True)

    def backward(n, carry):
        span = pl.ds(pl.multiple_of(n * tile, tile), tile)
        back = lax.dot_general(
            right_ref[:, width:], two[span, :], (((1,), (1,)), ((), ())), preferred_element_type=f32
        ) * scale
        value = pre[:, span]
        sig = jax.nn.sigmoid(value)
        right_ref[:, span] = (back * (sig * (1.0 + value * (1.0 - sig)))).astype(bf16)
        return carry

    lax.fori_loop(0, parts, backward, 0, unroll=True)
    if keep:
        one_save.wait()
        two_save.wait()


def step(xy, one, two, rows_dev, keep, places, base):
    rows, width = xy.shape[0], xy.shape[1] // 2
    tile = 1024
    vmem = pl.BlockSpec(memory_space=pltpu.VMEM)
    hbm = pl.BlockSpec(memory_space=pl.ANY)
    out = jax.ShapeDtypeStruct((rows, 2 * width), bf16)
    whole = jax.ShapeDtypeStruct((2 * width, width), bf16)
    sources = [array for p in one + two for array in p[0]]

    def entries(pieces):
        return tuple((p[1], len(p[0]), *(p[2:] or (0, p[0][0].shape[0]))) for p in pieces)

    return pl.pallas_call(
        functools.partial(
            step_kernel, rows_dev, tile, keep, base, entries(one), entries(two)
        ),
        out_shape=(out, out) + ((whole,) if keep else ()),
        in_specs=[pl.BlockSpec(memory_space=pltpu.SMEM), vmem] + [hbm] * len(sources),
        out_specs=(vmem, vmem) + ((hbm,) if keep else ()),
        scratch_shapes=[
            pltpu.VMEM((width, width), bf16),
            pltpu.VMEM((width, width), bf16),
            pltpu.VMEM((rows, width), f32),
            pltpu.SemaphoreType.DMA((len(one), width // tile)),
            pltpu.SemaphoreType.DMA((len(two),)),
            pltpu.SemaphoreType.DMA((2,)),
        ],
        compiler_params=pltpu.CompilerParams(vmem_limit_bytes=STEP_VMEM if keep else TILE_VMEM),
        cost_estimate=pl.CostEstimate(flops=15 * rows * width * width, bytes_accessed=4 * width * width, transcendentals=0),
    )(places, xy, *sources)


def update_kernel(guard, tile, a_ref, b_ref, p_ref, out_ref):
    shrink = inner_rate * decay
    turned = a_ref[...].T
    for n in range(p_ref.shape[1] // tile):
        span = slice(n * tile, (n + 1) * tile)
        grad = jnp.dot(turned, b_ref[:, span], preferred_element_type=f32)
        move = grad * pl.reciprocal(jnp.abs(grad) + guard, approx=True)
        out_ref[:, span] = (p_ref[:, span].astype(f32) * (1.0 - shrink) - inner_rate * move).astype(bf16)


def update(left, right, start, guard):
    rows, width = left.shape[0], start.shape[1]
    tall = 512
    each = width // tall
    return pl.pallas_call(
        functools.partial(update_kernel, guard * width ** 0.5, 512),
        out_shape=jax.ShapeDtypeStruct(start.shape, bf16),
        grid=(2 * each,),
        in_specs=[
            pl.BlockSpec((rows, tall), lambda m: (0, m)),
            pl.BlockSpec((rows, width), lambda m: (0, m // each)),
            pl.BlockSpec((tall, width), lambda m: (m, 0)),
        ],
        out_specs=pl.BlockSpec((tall, width), lambda m: (m, 0)),
        compiler_params=pltpu.CompilerParams(vmem_limit_bytes=TILE_VMEM),
        cost_estimate=pl.CostEstimate(flops=12 * rows * width * start.shape[0], bytes_accessed=4 * start.size, transcendentals=0),
    )(left, right, start)


def term_kernel(guard, tile, base, spans, place_ref, weight_ref, a_ref, b_ref, c_ref, d_ref, p_ref, *refs):
    outs, held, sem = refs[:-2], refs[-2], refs[-1]
    step = pl.program_id(0)
    slot = step % 2
    last = spans[-1][1]
    short, wide = p_ref.shape

    def copies(m, slot):
        return [
            (
                (m >= begin) & (m < end),
                pltpu.make_async_copy(
                    held.at[slot], out.at[pl.ds(pl.multiple_of((m - begin) * short, short), short), :], sem.at[slot]
                ),
            )
            for out, (begin, end) in zip(outs, spans)
        ]

    def settle(slot):
        pltpu.make_async_copy(held.at[slot], outs[0].at[pl.ds(0, short), :], sem.at[slot]).wait()

    @pl.when(step >= 2)
    def _():
        settle(slot)

    weight = jnp.where(place_ref[base + 3 * last + step] == 0, weight_ref[0], weight_ref[1])
    shrink = inner_rate * decay
    new_m = (1.0 - beta_one) / (1.0 - beta_one ** 2)
    new_v = ((1.0 - beta_two) / (1.0 - beta_two ** 2)) ** 0.5
    by_first = weight * (inner_rate * (1.0 - shrink))
    by_second = weight * (inner_rate * new_m / new_v)
    by_start = weight * (shrink * (2.0 - shrink))
    older, newer = a_ref[...].T, c_ref[...].T
    for n in range(wide // tile):
        span = slice(n * tile, (n + 1) * tile)
        old = jnp.dot(older, b_ref[:, span], preferred_element_type=f32)
        new = jnp.dot(newer, d_ref[:, span], preferred_element_type=f32)
        first = old * pl.reciprocal(jnp.abs(old) + guard, approx=True)
        square = beta_two * (old * old) + new * new
        root = square * lax.rsqrt(square + 1e-30)
        second = (beta_one * old + new) * pl.reciprocal(root + guard / new_v, approx=True)
        start = p_ref[:, span].astype(f32)
        held[slot, :, span] = (first * by_first + second * by_second + start * by_start).astype(bf16)
    for here, copy in copies(step, slot):
        pl.when(here)(copy.start)

    @pl.when(step == last - 1)
    def _():
        settle(slot)
        if last > 1:
            settle(1 - slot)


def terms(weights, places, base, counts, short, parts, a, b, c, d, p, guard):
    rows, width = a.shape[0], p.shape[1]
    wide = width // parts
    ends = [sum(counts[: n + 1]) for n in range(len(counts))]
    spans = tuple((end - count, end) for count, end in zip(counts, ends))
    last = ends[-1]
    row = lambda m, at: at[base + m]
    col = lambda m, at: at[base + last + m]
    both = lambda m, at: at[base + 2 * last + m]
    side = pl.BlockSpec((rows, short), lambda m, at: (0, row(m, at)))
    full = pl.BlockSpec((rows, wide), lambda m, at: (0, both(m, at)))
    return pl.pallas_call(
        functools.partial(term_kernel, guard * width ** 0.5, 256, base, spans),
        out_shape=tuple(jax.ShapeDtypeStruct((count * short, wide), bf16) for count in counts),
        grid_spec=pltpu.PrefetchScalarGridSpec(
            num_scalar_prefetch=1,
            grid=(last,),
            in_specs=[
                pl.BlockSpec(memory_space=pltpu.SMEM),
                side, full, side, full,
                pl.BlockSpec((short, wide), lambda m, at: (row(m, at), col(m, at))),
            ],
            out_specs=tuple(pl.BlockSpec(memory_space=pl.ANY) for _ in counts),
            scratch_shapes=[pltpu.VMEM((2, short, wide), bf16), pltpu.SemaphoreType.DMA((2,))],
        ),
        compiler_params=pltpu.CompilerParams(vmem_limit_bytes=TILE_VMEM),
        cost_estimate=pl.CostEstimate(flops=1, bytes_accessed=1, transcendentals=0),
    )(places, weights, a, b, c, d, p)


def slots(routes, documents, targets, device_of, room):
    dest = device_of(routes[:, 0])
    paths = device_of(None)
    hit = (dest[:, None] == jnp.arange(paths, dtype=jnp.int32)[None, :]).astype(jnp.int32)
    before = jnp.cumsum(hit, axis=0) - hit
    slot = dest * room + jnp.sum(before * hit, axis=1)
    place = (slot[:, None] == jnp.arange(paths * room, dtype=jnp.int32)[None, :]).astype(bf16)
    both = jnp.concatenate([documents, targets], axis=1)
    return jnp.einsum("rs,rd->sd", place, both, preferred_element_type=f32).astype(bf16)


def after(value, *others):
    return lax.optimization_barrier((value,) + others)[0]


def shards(documents, targets, routes, doc_counts, module_one, module_two, moment_one, moment_two):
    n_row = lax.axis_size("row")
    n_col = lax.axis_size("col")
    chips, half = n_row // 2, n_col // 2
    paths = n_row * n_col
    row_id = lax.axis_index("row")
    col_id = lax.axis_index("col")
    chip, core = row_id // 2, row_id % 2
    side, turn = col_id // half, col_id % half
    home = core == side
    micro, rows_dev, width = documents.shape
    room = max(2, 2 * rows_dev // paths)
    guard = 0.5 / (width * rows_dev) ** 0.5

    def device_of(path):
        if path is None:
            return paths
        i, j = path // n_col, path % n_col
        return (2 * (i // 2) + j // half) * n_col + (i % 2) * half + j % half

    def send(value, target):
        pairs = []
        for i in range(n_row):
            for k in range(n_col):
                to = target(i // 2, i % 2, k // half, k % half)
                if to is not None:
                    c, b, h, q = to
                    pairs.append((i * n_col + k, (2 * c + b) * n_col + h * half + q))
        return lax.ppermute(value, ("row", "col"), pairs)

    def to_core(value):
        return send(value, lambda c, b, h, q: (c, 1 - b, h, q))

    def to_turn(value, s):
        return send(value, lambda c, b, h, q: (c, b, h, (q + s) % half))

    def to_chip(value, bit):
        return send(value, lambda c, b, h, q: (c ^ bit, b, h, q))

    bits = [1 << t for t in range(chips.bit_length() - 1)]
    orders = [bits, bits[::-1]]
    cols = width // 2

    every = list(range(chips))
    tall_one, tall_two = width // n_col, width // chips
    short = min(tall_one, tall_two, 512)
    table = []

    def enter(*pieces):
        talls = (tall_one, tall_two)
        listed = [
            (
                level * (width // short) + block * (talls[level] // short) + cut,
                part,
                level * 2 + part,
                level,
            )
            for level, blocks, part in pieces
            for block in blocks
            for cut in range(talls[level] // short)
        ]
        base = len(table)
        for field in zip(*listed):
            table.extend(field)
        return base, tuple(len(blocks) * (talls[level] // short) for level, blocks, part in pieces)

    here = [(turn + s) % half + core * half for s in range(half)]
    there = [(turn + s) % half + (1 - core) * half for s in range(half)]
    leave = [[chip ^ r for r in every if r & order[0]] for order in orders]
    stay = [[chip ^ r for r in every if not r & order[0]] for order in orders]
    calls = [
        enter((0, there, 0), (0, there, 1)),
        enter((0, here, 0), (0, here, 1)),
        enter((1, leave[0], 0), (1, leave[1], 1)),
        enter((1, stay[0], 0), (1, stay[1], 1)),
    ]
    base_first = len(table)
    for part in range(2):
        for other in (core, 1 - core):
            table += [(turn - s) % half + other * half for s in range(half)]
    for order in orders:
        held = [0]
        for bit in order:
            held = held + [r ^ bit for r in held]
        table += [chip ^ r for r in held]
    table.append(home)
    base_second = len(table)
    table += [0, 0, 0]
    places = jnp.stack([jnp.asarray(value).astype(jnp.int32) for value in table])

    counts = doc_counts.astype(f32)
    path_one, path_two = 2 * chip + side, turn + core * half
    in_row = (jnp.arange(n_row) == path_one)[:, None]
    in_col = (jnp.arange(n_col) == path_two)[None, :]
    row_counts = jnp.sum(jnp.where(in_row, counts, 0.0))
    col_counts = jnp.sum(jnp.where(in_col, counts, 0.0))
    own_count = jnp.sum(jnp.where(in_row & in_col, counts, 0.0))
    weights = jnp.stack([own_count / row_counts, own_count / col_counts])

    sent = [slots(routes[s], documents[s], targets[s], device_of, room) for s in range(micro)]

    def exchange(value):
        return lax.all_to_all(
            value.reshape(paths, room, 2 * width), ("row", "col"), split_axis=0, concat_axis=0, tiled=True
        ).reshape(paths * room, 2 * width)

    own_two = module_two[0].astype(bf16)
    own_one = module_one[0].astype(bf16)
    other_two = send(own_two, lambda c, b, h, q: (c, h, h, q) if b != h else None)
    pair_two = jnp.where(
        core == 0,
        jnp.concatenate([own_two, other_two], axis=0),
        jnp.concatenate([other_two, own_two], axis=0),
    )

    def to_chips(value, bit, here):
        return send(value, lambda c, b, h, q: (c ^ bit, b, h, q) if (b == h) == here else None)

    def to_half(value, here):
        if half == 1:
            return jnp.zeros_like(value)
        return send(value, lambda c, b, h, q: (c, b, h, (q + 1) % half) if (b == h) == here else None)

    def begin(pair, here):
        own = [pair[:, part * cols : (part + 1) * cols] for part in range(2)]
        return [(value, to_chips(value, order[0], here)) for value, order in zip(own, orders)]

    def proceed(held, here):
        for n in range(1, len(bits)):
            held = [jnp.concatenate(pieces, axis=0) for pieces in held]
            held = [(value, to_chips(value, order[n], here)) for value, order in zip(held, orders)]
        return held

    def barrier(*values):
        return jax.tree.unflatten(jax.tree.structure(values), lax.optimization_barrier(jax.tree.leaves(values)))

    ones = [own_one[:, :cols], own_one[:, cols:]]

    def far_half(value):
        return send(value, lambda c, b, h, q: (c, 1 - b, 1 - h, q) if b != h else None)

    fars, nears = [far_half(ones[0])], [to_half(ones[0], True)]
    home_two = begin(pair_two, True)
    ones, fars, nears, pair_two, places, weights, sent = barrier(
        ones, fars, nears, pair_two, places, weights, sent
    )
    far_two = send(pair_two, lambda c, b, h, q: (c, b, 1 - h, q) if b == h else None)
    turns = [to_half(fars[0], False)]
    home_two = proceed(home_two, True)
    ones, fars, nears, turns, far_two, home_two, sent = barrier(ones, fars, nears, turns, far_two, home_two, sent)
    fars.append(far_half(ones[1]))
    nears.append(to_half(ones[1], True))
    away_two = begin(far_two, False)
    fars, nears, away_two, sent = barrier(fars, nears, away_two, sent)
    got_a = exchange(sent[0])
    turns.append(to_half(fars[1], False))
    away_two = proceed(away_two, False)
    one = []
    for part in range(2):
        held = [jnp.where(home, ones[part], fars[part])]
        if half > 1:
            held.append(jnp.where(home, nears[part], turns[part]))
        held += [to_turn(held[0], s) for s in range(2, half)]
        joined = jnp.concatenate(held, axis=0)
        for value in (joined, to_core(joined)):
            one += [((value,), part * cols, s * tall_one, tall_one) for s in range(half)]
    two = []
    for part in range(2):
        for mine, theirs in zip(home_two[part], away_two[part]):
            count = mine.shape[0] // tall_two
            two += [((mine, theirs), part * cols, n * tall_two, tall_two) for n in range(count)]
    got_b = exchange(after(sent[1], got_a, away_two[0][1], away_two[1][1]))
    left_a, right_a, start = step(got_a, one, two, rows_dev, True, places, base_first)
    moved = update(left_a, right_a, start, guard)
    left_b, right_b = step(got_b, [((moved,), 0, 0, width)], [((moved,), 0, width, width)], rows_dev, False, places, base_second)

    def deltas(call, *others):
        return terms(after(weights, *others), places, *call, short, 2, left_a, right_a, left_b, right_b, start, guard)

    def summed(*values):
        return functools.reduce(lambda x, y: x + y, [value.astype(f32) for value in values])

    def both_cores(here, there):
        there = to_core(there)
        cuts = [slice(s * tall_one, (s + 1) * tall_one) for s in range(half)]
        return [(here[cut], there[cut]) for cut in cuts]

    def along(both, sums):
        return [*both[0], *[to_turn(value, s) for s, value in enumerate(sums, 1)]]

    def to_owner(terms, *others):
        return send(
            after(summed(*terms).astype(bf16), *others),
            lambda c, b, h, q: (c, 1 - b, 1 - h, q) if b != h else None,
        )

    def chip_sum(part, here, there):
        there = to_chip(there, orders[part][0])
        cuts = [slice(n * tall_two, (n + 1) * tall_two) for n in range(chips // 2)]
        left = [r for r in every if not r & orders[part][0]]
        return {r: [here[cut], there[cut]] for r, cut in zip(left, cuts)}

    def chip_rest(part, held, *others):
        held = {r: list(pieces) for r, pieces in held.items()}
        for bit in orders[part][1:]:
            for r in [r for r in sorted(held) if r & bit]:
                held[r ^ bit].append(to_chip(after(summed(*held.pop(r)).astype(bf16), *others), bit))
        return held[0]

    def half_sum(terms, *others):
        total = summed(*terms)
        up, down = total[: tall_two // 2], total[tall_two // 2 :]
        near = send(
            jnp.where(core == 0, down, up).astype(bf16),
            lambda c, b, h, q: (c, 1 - b, h, q) if b == h else None,
        )
        fars = [
            send(
                after(rows.astype(bf16), *others),
                lambda c, b, h, q, to=to: (c, to, 1 - h, q) if b != h else None,
            )
            for to, rows in enumerate((up, down))
        ]
        return jnp.where(home, jnp.where(core == 0, up, down), near.astype(f32)) + jnp.where(
            core == 0, *[far.astype(f32) for far in fars]
        )

    def outer(module, moment, sums):
        average = jnp.concatenate(sums, axis=1)[None]
        following = outer_moment * moment + average
        return module - outer_rate * (outer_moment * following + average), following

    there_a, there_b = deltas(calls[0])
    here_a, here_b = deltas(calls[1], there_a)
    both_a, both_b = both_cores(here_a, there_a), both_cores(here_b, there_b)
    sums_a, sums_b = ([summed(*pair).astype(bf16) for pair in both[1:]] for both in (both_a, both_b))
    leave_a, leave_b = deltas(calls[2], here_a, *sums_a, *sums_b)
    along_a, along_b = along(both_a, sums_a), along(both_b, sums_b)
    stay_a, stay_b = deltas(calls[3], leave_a, along_a[-1])
    owned_a = to_owner(along_a)
    owned_b = to_owner(along_b, stay_a)
    chip_a, chip_b = chip_sum(0, stay_a, leave_a), chip_sum(1, stay_b, leave_b)
    chip_a, chip_b = chip_rest(0, chip_a, owned_a), chip_rest(1, chip_b, owned_a)
    sums_one = [
        jnp.where(home, summed(*terms), owned.astype(f32))
        for terms, owned in ((along_a, owned_a), (along_b, owned_b))
    ]
    new_one, next_moment_one = outer(module_one, moment_one, sums_one)
    sums_two = [half_sum(terms, owned_b) for terms in (chip_a, chip_b)]
    new_two, next_moment_two = outer(module_two, moment_two, sums_two)
    return (new_one, new_two, next_moment_one, next_moment_two)


def solution(mesh):
    return jax.shard_map(
        shards,
        mesh=mesh,
        in_specs=(
            P(None, ("row", "col"), None),
            P(None, ("row", "col"), None),
            P(None, ("row", "col"), None),
            P(),
            P("row", "col", None),
            P("col", "row", None),
            P("row", "col", None),
            P("col", "row", None),
        ),
        out_specs=(
            P("row", "col", None),
            P("col", "row", None),
            P("row", "col", None),
            P("col", "row", None),
        ),
        check_vma=False,
    )
```

```python
import functools

import jax
import jax.numpy as jnp
from jax import lax
from jax.experimental import pallas as pl
from jax.experimental.pallas import tpu as pltpu
from jax.sharding import PartitionSpec as P

beta_one = 0.9
beta_two = 0.95
inner_rate = 0.1
decay = 0.1
outer_rate = 0.7
outer_moment = 0.9

STEP_VMEM = 63 * 1024 * 1024
TILE_VMEM = 32 * 1024 * 1024
f32 = jnp.float32
bf16 = jnp.bfloat16


def step_kernel(rows_dev, tile, keep, base, one_at, two_at, *refs):
    n_one, n_two = len(one_at), len(two_at)
    place_ref, xy_ref = refs[:2]
    refs = refs[2:]

    def take(places):
        nonlocal refs
        found = [tuple(refs[sum(p[1] for p in places[:i]) :][: p[1]]) for i, p in enumerate(places)]
        refs = refs[sum(p[1] for p in places) :]
        return found

    one_refs, two_refs = take(one_at), take(two_at)
    left_ref, right_ref = refs[:2]
    start_out = refs[2] if keep else None
    one, two, pre, one_sem, two_sem, out_sem = refs[-6:]
    width = one.shape[0]
    scale = width ** (-0.5)
    parts = width // tile
    home = place_ref[base + n_one + n_two]

    class Copies:
        def __init__(self, *choices):
            self.choices = choices

        def start(self):
            if len(self.choices) == 1:
                self.choices[0].start()
            else:
                pl.when(home == 1)(self.choices[0].start)
                pl.when(home == 0)(self.choices[1].start)

        def wait(self):
            self.choices[0].wait()

    def one_copies(n):
        found = []
        for i, (pieces, (first, _, top, tall)) in enumerate(zip(one_refs, one_at)):
            wide = pieces[0].shape[1]
            if first <= n * tile < first + wide:
                down = pl.ds(pl.multiple_of(place_ref[base + i] * tall, tall), tall)
                found.append(
                    Copies(*[
                        pltpu.make_async_copy(
                            piece.at[pl.ds(top, tall), pl.ds(n * tile - first, tile)],
                            one.at[down, pl.ds(n * tile, tile)],
                            one_sem.at[i, n],
                        )
                        for piece in pieces
                    ])
                )
        return found

    two_copies = []
    for i, (pieces, (first, _, top, tall)) in enumerate(zip(two_refs, two_at)):
        wide = pieces[0].shape[1]
        down = pl.ds(pl.multiple_of(place_ref[base + n_one + i] * tall, tall), tall)
        two_copies.append(
            Copies(*[
                pltpu.make_async_copy(piece.at[pl.ds(top, tall), :], two.at[down, pl.ds(first, wide)], two_sem.at[i])
                for piece in pieces
            ])
        )
    for n in range(parts):
        for copy in one_copies(n):
            copy.start()
    for copy in two_copies:
        copy.start()
    for n in range(parts):
        span = pl.ds(n * tile, tile)
        for copy in one_copies(n):
            copy.wait()
        value = jnp.dot(xy_ref[:, :width], one[:, span], preferred_element_type=f32) * scale
        pre[:, span] = value
        left_ref[:, span] = xy_ref[:, span]
        left_ref[:, pl.ds(width + n * tile, tile)] = (value * jax.nn.sigmoid(value)).astype(bf16)
    for copy in two_copies:
        copy.wait()
    if keep:
        one_save = pltpu.make_async_copy(one, start_out.at[pl.ds(0, width), :], out_sem.at[0])
        two_save = pltpu.make_async_copy(two, start_out.at[pl.ds(width, width), :], out_sem.at[1])
        one_save.start()
        two_save.start()

    def miss(n, carry):
        span = pl.ds(pl.multiple_of(n * tile, tile), tile)
        late = pl.ds(pl.multiple_of(width + n * tile, tile), tile)
        out = xy_ref[:, span].astype(f32) + jnp.dot(left_ref[:, width:], two[:, span], preferred_element_type=f32) * scale
        right_ref[:, late] = ((out - xy_ref[:, late].astype(f32)) / rows_dev).astype(bf16)
        return carry

    lax.fori_loop(0, parts, miss, 0, unroll=True)

    def backward(n, carry):
        span = pl.ds(pl.multiple_of(n * tile, tile), tile)
        back = lax.dot_general(
            right_ref[:, width:], two[span, :], (((1,), (1,)), ((), ())), preferred_element_type=f32
        ) * scale
        value = pre[:, span]
        sig = jax.nn.sigmoid(value)
        right_ref[:, span] = (back * (sig * (1.0 + value * (1.0 - sig)))).astype(bf16)
        return carry

    lax.fori_loop(0, parts, backward, 0, unroll=True)
    if keep:
        one_save.wait()
        two_save.wait()


def step(xy, one, two, rows_dev, keep, places, base):
    rows, width = xy.shape[0], xy.shape[1] // 2
    tile = 1024
    vmem = pl.BlockSpec(memory_space=pltpu.VMEM)
    hbm = pl.BlockSpec(memory_space=pl.ANY)
    out = jax.ShapeDtypeStruct((rows, 2 * width), bf16)
    whole = jax.ShapeDtypeStruct((2 * width, width), bf16)
    sources = [array for p in one + two for array in p[0]]

    def entries(pieces):
        return tuple((p[1], len(p[0]), *(p[2:] or (0, p[0][0].shape[0]))) for p in pieces)

    return pl.pallas_call(
        functools.partial(
            step_kernel, rows_dev, tile, keep, base, entries(one), entries(two)
        ),
        out_shape=(out, out) + ((whole,) if keep else ()),
        in_specs=[pl.BlockSpec(memory_space=pltpu.SMEM), vmem] + [hbm] * len(sources),
        out_specs=(vmem, vmem) + ((hbm,) if keep else ()),
        scratch_shapes=[
            pltpu.VMEM((width, width), bf16),
            pltpu.VMEM((width, width), bf16),
            pltpu.VMEM((rows, width), f32),
            pltpu.SemaphoreType.DMA((len(one), width // tile)),
            pltpu.SemaphoreType.DMA((len(two),)),
            pltpu.SemaphoreType.DMA((2,)),
        ],
        compiler_params=pltpu.CompilerParams(vmem_limit_bytes=STEP_VMEM if keep else TILE_VMEM),
        cost_estimate=pl.CostEstimate(flops=15 * rows * width * width, bytes_accessed=4 * width * width, transcendentals=0),
    )(places, xy, *sources)


def update_kernel(guard, tile, a_ref, b_ref, p_ref, out_ref):
    shrink = inner_rate * decay
    turned = a_ref[...].T
    for n in range(p_ref.shape[1] // tile):
        span = slice(n * tile, (n + 1) * tile)
        grad = jnp.dot(turned, b_ref[:, span], preferred_element_type=f32)
        move = grad * pl.reciprocal(jnp.abs(grad) + guard, approx=True)
        out_ref[:, span] = (p_ref[:, span].astype(f32) * (1.0 - shrink) - inner_rate * move).astype(bf16)


def update(left, right, start, guard):
    rows, width = left.shape[0], start.shape[1]
    tall = 512
    each = width // tall
    return pl.pallas_call(
        functools.partial(update_kernel, guard * width ** 0.5, 512),
        out_shape=jax.ShapeDtypeStruct(start.shape, bf16),
        grid=(2 * each,),
        in_specs=[
            pl.BlockSpec((rows, tall), lambda m: (0, m)),
            pl.BlockSpec((rows, width), lambda m: (0, m // each)),
            pl.BlockSpec((tall, width), lambda m: (m, 0)),
        ],
        out_specs=pl.BlockSpec((tall, width), lambda m: (m, 0)),
        compiler_params=pltpu.CompilerParams(vmem_limit_bytes=TILE_VMEM),
        cost_estimate=pl.CostEstimate(flops=12 * rows * width * start.shape[0], bytes_accessed=4 * start.size, transcendentals=0),
    )(left, right, start)


def term_kernel(guard, tile, base, spans, place_ref, weight_ref, a_ref, b_ref, c_ref, d_ref, p_ref, *refs):
    outs, held, sem = refs[:-2], refs[-2], refs[-1]
    step = pl.program_id(0)
    slot = step % 2
    last = spans[-1][1]
    short, wide = p_ref.shape

    def copies(m, slot):
        return [
            (
                (m >= begin) & (m < end),
                pltpu.make_async_copy(
                    held.at[slot], out.at[pl.ds(pl.multiple_of((m - begin) * short, short), short), :], sem.at[slot]
                ),
            )
            for out, (begin, end) in zip(outs, spans)
        ]

    def settle(slot):
        pltpu.make_async_copy(held.at[slot], outs[0].at[pl.ds(0, short), :], sem.at[slot]).wait()

    @pl.when(step >= 2)
    def _():
        settle(slot)

    weight = jnp.where(place_ref[base + 3 * last + step] == 0, weight_ref[0], weight_ref[1])
    shrink = inner_rate * decay
    new_m = (1.0 - beta_one) / (1.0 - beta_one ** 2)
    new_v = ((1.0 - beta_two) / (1.0 - beta_two ** 2)) ** 0.5
    by_first = weight * (inner_rate * (1.0 - shrink))
    by_second = weight * (inner_rate * new_m / new_v)
    by_start = weight * (shrink * (2.0 - shrink))
    older, newer = a_ref[...].T, c_ref[...].T
    for n in range(wide // tile):
        span = slice(n * tile, (n + 1) * tile)
        old = jnp.dot(older, b_ref[:, span], preferred_element_type=f32)
        new = jnp.dot(newer, d_ref[:, span], preferred_element_type=f32)
        first = old * pl.reciprocal(jnp.abs(old) + guard, approx=True)
        square = beta_two * (old * old) + new * new
        root = square * lax.rsqrt(square + 1e-30)
        second = (beta_one * old + new) * pl.reciprocal(root + guard / new_v, approx=True)
        start = p_ref[:, span].astype(f32)
        held[slot, :, span] = (first * by_first + second * by_second + start * by_start).astype(bf16)
    for here, copy in copies(step, slot):
        pl.when(here)(copy.start)

    @pl.when(step == last - 1)
    def _():
        settle(slot)
        if last > 1:
            settle(1 - slot)


def terms(weights, places, base, counts, short, parts, a, b, c, d, p, guard):
    rows, width = a.shape[0], p.shape[1]
    wide = width // parts
    ends = [sum(counts[: n + 1]) for n in range(len(counts))]
    spans = tuple((end - count, end) for count, end in zip(counts, ends))
    last = ends[-1]
    row = lambda m, at: at[base + m]
    col = lambda m, at: at[base + last + m]
    both = lambda m, at: at[base + 2 * last + m]
    side = pl.BlockSpec((rows, short), lambda m, at: (0, row(m, at)))
    full = pl.BlockSpec((rows, wide), lambda m, at: (0, both(m, at)))
    return pl.pallas_call(
        functools.partial(term_kernel, guard * width ** 0.5, 256, base, spans),
        out_shape=tuple(jax.ShapeDtypeStruct((count * short, wide), bf16) for count in counts),
        grid_spec=pltpu.PrefetchScalarGridSpec(
            num_scalar_prefetch=1,
            grid=(last,),
            in_specs=[
                pl.BlockSpec(memory_space=pltpu.SMEM),
                side, full, side, full,
                pl.BlockSpec((short, wide), lambda m, at: (row(m, at), col(m, at))),
            ],
            out_specs=tuple(pl.BlockSpec(memory_space=pl.ANY) for _ in counts),
            scratch_shapes=[pltpu.VMEM((2, short, wide), bf16), pltpu.SemaphoreType.DMA((2,))],
        ),
        compiler_params=pltpu.CompilerParams(vmem_limit_bytes=TILE_VMEM),
        cost_estimate=pl.CostEstimate(flops=1, bytes_accessed=1, transcendentals=0),
    )(places, weights, a, b, c, d, p)


def slots(routes, documents, targets, device_of, room):
    dest = device_of(routes[:, 0])
    paths = device_of(None)
    hit = (dest[:, None] == jnp.arange(paths, dtype=jnp.int32)[None, :]).astype(jnp.int32)
    before = jnp.cumsum(hit, axis=0) - hit
    slot = dest * room + jnp.sum(before * hit, axis=1)
    place = (slot[:, None] == jnp.arange(paths * room, dtype=jnp.int32)[None, :]).astype(bf16)
    both = jnp.concatenate([documents, targets], axis=1)
    return jnp.einsum("rs,rd->sd", place, both, preferred_element_type=f32).astype(bf16)


def after(value, *others):
    return lax.optimization_barrier((value,) + others)[0]


def shards(documents, targets, routes, doc_counts, module_one, module_two, moment_one, moment_two):
    n_row = lax.axis_size("row")
    n_col = lax.axis_size("col")
    chips, half = n_row // 2, n_col // 2
    paths = n_row * n_col
    row_id = lax.axis_index("row")
    col_id = lax.axis_index("col")
    chip, core = row_id // 2, row_id % 2
    side, turn = col_id // half, col_id % half
    home = core == side
    micro, rows_dev, width = documents.shape
    room = max(2, 2 * rows_dev // paths)
    guard = 0.5 / (width * rows_dev) ** 0.5

    def device_of(path):
        if path is None:
            return paths
        i, j = path // n_col, path % n_col
        return (2 * (i // 2) + j // half) * n_col + (i % 2) * half + j % half

    def send(value, target):
        pairs = []
        for i in range(n_row):
            for k in range(n_col):
                to = target(i // 2, i % 2, k // half, k % half)
                if to is not None:
                    c, b, h, q = to
                    pairs.append((i * n_col + k, (2 * c + b) * n_col + h * half + q))
        return lax.ppermute(value, ("row", "col"), pairs)

    def to_core(value):
        return send(value, lambda c, b, h, q: (c, 1 - b, h, q))

    def to_turn(value, s):
        return send(value, lambda c, b, h, q: (c, b, h, (q + s) % half))

    def to_chip(value, bit):
        return send(value, lambda c, b, h, q: (c ^ bit, b, h, q))

    bits = [1 << t for t in range(chips.bit_length() - 1)]
    orders = [bits, bits[::-1]]
    cols = width // 2

    every = list(range(chips))
    tall_one, tall_two = width // n_col, width // chips
    short = min(tall_one, tall_two, 512)
    table = []

    def enter(*pieces):
        talls = (tall_one, tall_two)
        listed = [
            (
                level * (width // short) + block * (talls[level] // short) + cut,
                part,
                level * 2 + part,
                level,
            )
            for level, blocks, part in pieces
            for block in blocks
            for cut in range(talls[level] // short)
        ]
        base = len(table)
        for field in zip(*listed):
            table.extend(field)
        return base, tuple(len(blocks) * (talls[level] // short) for level, blocks, part in pieces)

    here = [(turn + s) % half + core * half for s in range(half)]
    there = [(turn + s) % half + (1 - core) * half for s in range(half)]
    leave = [[chip ^ r for r in every if r & order[0]] for order in orders]
    stay = [[chip ^ r for r in every if not r & order[0]] for order in orders]
    calls = [
        enter((0, there, 0), (0, there, 1)),
        enter((0, here, 0), (0, here, 1)),
        enter((1, leave[0], 0), (1, leave[1], 1)),
        enter((1, stay[0], 0), (1, stay[1], 1)),
    ]
    base_first = len(table)
    for part in range(2):
        for other in (core, 1 - core):
            table += [(turn - s) % half + other * half for s in range(half)]
    for order in orders:
        held = [0]
        for bit in order:
            held = held + [r ^ bit for r in held]
        table += [chip ^ r for r in held]
    table.append(home)
    base_second = len(table)
    table += [0, 0, 0]
    places = jnp.stack([jnp.asarray(value).astype(jnp.int32) for value in table])

    counts = doc_counts.astype(f32)
    path_one, path_two = 2 * chip + side, turn + core * half
    in_row = (jnp.arange(n_row) == path_one)[:, None]
    in_col = (jnp.arange(n_col) == path_two)[None, :]
    row_counts = jnp.sum(jnp.where(in_row, counts, 0.0))
    col_counts = jnp.sum(jnp.where(in_col, counts, 0.0))
    own_count = jnp.sum(jnp.where(in_row & in_col, counts, 0.0))
    weights = jnp.stack([own_count / row_counts, own_count / col_counts])

    sent = [slots(routes[s], documents[s], targets[s], device_of, room) for s in range(micro)]

    def exchange(value):
        return lax.all_to_all(
            value.reshape(paths, room, 2 * width), ("row", "col"), split_axis=0, concat_axis=0, tiled=True
        ).reshape(paths * room, 2 * width)

    own_two = module_two[0].astype(bf16)
    own_one = module_one[0].astype(bf16)
    other_two = send(own_two, lambda c, b, h, q: (c, h, h, q) if b != h else None)
    pair_two = jnp.where(
        core == 0,
        jnp.concatenate([own_two, other_two], axis=0),
        jnp.concatenate([other_two, own_two], axis=0),
    )

    def to_chips(value, bit, here):
        return send(value, lambda c, b, h, q: (c ^ bit, b, h, q) if (b == h) == here else None)

    def to_half(value, here):
        if half == 1:
            return jnp.zeros_like(value)
        return send(value, lambda c, b, h, q: (c, b, h, (q + 1) % half) if (b == h) == here else None)

    def begin(pair, here):
        own = [pair[:, part * cols : (part + 1) * cols] for part in range(2)]
        return [(value, to_chips(value, order[0], here)) for value, order in zip(own, orders)]

    def proceed(held, here):
        for n in range(1, len(bits)):
            held = [jnp.concatenate(pieces, axis=0) for pieces in held]
            held = [(value, to_chips(value, order[n], here)) for value, order in zip(held, orders)]
        return held

    def barrier(*values):
        return jax.tree.unflatten(jax.tree.structure(values), lax.optimization_barrier(jax.tree.leaves(values)))

    ones = [own_one[:, :cols], own_one[:, cols:]]

    def far_half(value):
        return send(value, lambda c, b, h, q: (c, 1 - b, 1 - h, q) if b != h else None)

    fars, nears = [far_half(ones[0])], [to_half(ones[0], True)]
    home_two = begin(pair_two, True)
    ones, fars, nears, pair_two, places, weights, sent = barrier(
        ones, fars, nears, pair_two, places, weights, sent
    )
    far_two = send(pair_two, lambda c, b, h, q: (c, b, 1 - h, q) if b == h else None)
    turns = [to_half(fars[0], False)]
    home_two = proceed(home_two, True)
    ones, fars, nears, turns, far_two, home_two, sent = barrier(ones, fars, nears, turns, far_two, home_two, sent)
    fars.append(far_half(ones[1]))
    nears.append(to_half(ones[1], True))
    away_two = begin(far_two, False)
    fars, nears, away_two, sent = barrier(fars, nears, away_two, sent)
    got_a = exchange(sent[0])
    turns.append(to_half(fars[1], False))
    away_two = proceed(away_two, False)
    one = []
    for part in range(2):
        held = [jnp.where(home, ones[part], fars[part])]
        if half > 1:
            held.append(jnp.where(home, nears[part], turns[part]))
        held += [to_turn(held[0], s) for s in range(2, half)]
        joined = jnp.concatenate(held, axis=0)
        for value in (joined, to_core(joined)):
            one += [((value,), part * cols, s * tall_one, tall_one) for s in range(half)]
    two = []
    for part in range(2):
        for mine, theirs in zip(home_two[part], away_two[part]):
            count = mine.shape[0] // tall_two
            two += [((mine, theirs), part * cols, n * tall_two, tall_two) for n in range(count)]
    got_b = exchange(after(sent[1], got_a, away_two[0][1], away_two[1][1]))
    left_a, right_a, start = step(got_a, one, two, rows_dev, True, places, base_first)
    moved = update(left_a, right_a, start, guard)
    left_b, right_b = step(got_b, [((moved,), 0, 0, width)], [((moved,), 0, width, width)], rows_dev, False, places, base_second)

    def deltas(call, *others):
        return terms(after(weights, *others), places, *call, short, 2, left_a, right_a, left_b, right_b, start, guard)

    def summed(*values):
        return functools.reduce(lambda x, y: x + y, [value.astype(f32) for value in values])

    def both_cores(here, there):
        there = to_core(there)
        cuts = [slice(s * tall_one, (s + 1) * tall_one) for s in range(half)]
        return [(here[cut], there[cut]) for cut in cuts]

    def along(both, sums):
        return [*both[0], *[to_turn(value, s) for s, value in enumerate(sums, 1)]]

    def to_owner(terms, *others):
        return send(
            after(summed(*terms).astype(bf16), *others),
            lambda c, b, h, q: (c, 1 - b, 1 - h, q) if b != h else None,
        )

    def chip_sum(part, here, there):
        there = to_chip(there, orders[part][0])
        cuts = [slice(n * tall_two, (n + 1) * tall_two) for n in range(chips // 2)]
        left = [r for r in every if not r & orders[part][0]]
        return {r: [here[cut], there[cut]] for r, cut in zip(left, cuts)}

    def chip_rest(part, held, *others):
        held = {r: list(pieces) for r, pieces in held.items()}
        for bit in orders[part][1:]:
            for r in [r for r in sorted(held) if r & bit]:
                held[r ^ bit].append(to_chip(after(summed(*held.pop(r)).astype(bf16), *others), bit))
        return held[0]

    def half_sum(terms, *others):
        total = summed(*terms)
        up, down = total[: tall_two // 2], total[tall_two // 2 :]
        near = send(
            jnp.where(core == 0, down, up).astype(bf16),
            lambda c, b, h, q: (c, 1 - b, h, q) if b == h else None,
        )
        fars = [
            send(
                after(rows.astype(bf16), *others),
                lambda c, b, h, q, to=to: (c, to, 1 - h, q) if b != h else None,
            )
            for to, rows in enumerate((up, down))
        ]
        return jnp.where(home, jnp.where(core == 0, up, down), near.astype(f32)) + jnp.where(
            core == 0, *[far.astype(f32) for far in fars]
        )

    def outer(module, moment, sums):
        average = jnp.concatenate(sums, axis=1)[None]
        following = outer_moment * moment + average
        return module - outer_rate * (outer_moment * following + average), following

    there_a, there_b = deltas(calls[0])
    here_a, here_b = deltas(calls[1], there_a)
    both_a, both_b = both_cores(here_a, there_a), both_cores(here_b, there_b)
    sums_a, sums_b = ([summed(*pair).astype(bf16) for pair in both[1:]] for both in (both_a, both_b))
    leave_a, leave_b = deltas(calls[2], here_a, *sums_a, *sums_b)
    along_a, along_b = along(both_a, sums_a), along(both_b, sums_b)
    stay_a, stay_b = deltas(calls[3], leave_a, along_a[-1])
    owned_a = to_owner(along_a)
    owned_b = to_owner(along_b, stay_a)
    chip_a, chip_b = chip_sum(0, stay_a, leave_a), chip_sum(1, stay_b, leave_b)
    chip_a, chip_b = chip_rest(0, chip_a, owned_a), chip_rest(1, chip_b, owned_a)
    sums_one = [
        jnp.where(home, summed(*terms), owned.astype(f32))
        for terms, owned in ((along_a, owned_a), (along_b, owned_b))
    ]
    new_one, next_moment_one = outer(module_one, moment_one, sums_one)
    sums_two = [half_sum(terms, owned_b) for terms in (chip_a, chip_b)]
    new_two, next_moment_two = outer(module_two, moment_two, sums_two)
    return (new_one, new_two, next_moment_one, next_moment_two)


def solution(mesh):
    return jax.shard_map(
        shards,
        mesh=mesh,
        in_specs=(
            P(None, ("row", "col"), None),
            P(None, ("row", "col"), None),
            P(None, ("row", "col"), None),
            P(),
            P("row", "col", None),
            P("col", "row", None),
            P("row", "col", None),
            P("col", "row", None),
        ),
        out_specs=(
            P("row", "col", None),
            P("col", "row", None),
            P("row", "col", None),
            P("col", "row", None),
        ),
        check_vma=False,
    )
```
